32 devices in a mesh: fsdp: 4 (over y, x), seq: 8 (over z, core).
Axes of the slice: x: 2, y: 2, z: 4, core: 2. Of those that a mesh axis runs over, the one named last changes fastest.
Arguments:
- layer_input: bfloat16 [8, 1024, 1024], P('fsdp', 'seq'), may hold values from -8 to 8
- documents: int32 [8, 1024], P('fsdp', 'seq'), may hold values from 0 to 5, as said below
- cotangent: bfloat16 [8, 1024, 1024], P('fsdp', 'seq'), may hold values from -6 to 6
- attend_weight: float32 [2, 3, 1024, 1024], P(None, None, ('fsdp', 'seq')), may hold values from -0.25 to 0.25
- attend_bias: float32 [2, 2, 1024], P(None, None, ('fsdp', 'seq')), may hold values from -3 to 3
- output_weight: float32 [2, 1024, 1024], P(None, ('fsdp', 'seq')), may hold values from -0.5 to 0.5
- output_bias: float32 [2, 1024], P(None, ('fsdp', 'seq')), may hold values from -3 to 3
- norm_gain: float32 [2, 2, 1024], P(None, None, ('fsdp', 'seq')), may hold values from 0.25 to 1.75
- norm_shift: float32 [2, 2, 1024], P(None, None, ('fsdp', 'seq')), may hold values from -1.75 to 1.75
- expand_weight: float32 [2, 1024, 4096], P(None, ('fsdp', 'seq')), may hold values from -0.1875 to 0.1875
- expand_bias: float32 [2, 4096], P(None, ('fsdp', 'seq')), may hold values from -3 to 3
- reduce_weight: float32 [2, 4096, 1024], P(None, ('fsdp', 'seq')), may hold values from -0.09375 to 0.09375
- reduce_bias: float32 [2, 1024], P(None, ('fsdp', 'seq')), may hold values from -3 to 3
Outputs:
- layer_output: bfloat16 [8, 1024, 1024], P('fsdp', 'seq')
- input_gradient: float32 [8, 1024, 1024], P('fsdp', 'seq')
- attend_weight_grad: float32 [2, 3, 1024, 1024], P(None, None, ('fsdp', 'seq'))
- attend_bias_grad: float32 [2, 2, 1024], P(None, None, ('fsdp', 'seq'))
- output_weight_grad: float32 [2, 1024, 1024], P(None, ('fsdp', 'seq'))
- output_bias_grad: float32 [2, 1024], P(None, ('fsdp', 'seq'))
- norm_gain_grad: float32 [2, 2, 1024], P(None, None, ('fsdp', 'seq'))
- norm_shift_grad: float32 [2, 2, 1024], P(None, None, ('fsdp', 'seq'))
- expand_weight_grad: float32 [2, 1024, 4096], P(None, ('fsdp', 'seq'))
- expand_bias_grad: float32 [2, 4096], P(None, ('fsdp', 'seq'))
- reduce_weight_grad: float32 [2, 4096, 1024], P(None, ('fsdp', 'seq'))
- reduce_bias_grad: float32 [2, 1024], P(None, ('fsdp', 'seq'))
The draws below stay inside these ranges and needn't reach their ends.
Inputs may be any that keep to these rules, and one draw needn't show every extreme that they name: In each sequence the numbers start at 0 and rise by one at the start of each document. Of the 2 sequences on each index of fsdp, one has a first document of fewer than 128 tokens and a second that runs to the sequence's end, so that it has 897 to 1023 tokens and is not bounded by 1500; another is made of documents of exactly 200 tokens. Every other document has 200 to 1500 tokens, except that the last of a sequence is cut at the sequence's end.
All inputs are finite; a program needn't handle non-finite values.
Results may differ from the reference program's by a relative error of at most 0.035.
The reference program's roundings to bfloat16 on the way count: a program that leaves them out, or rounds other values in their place, can miss the bound.
Values may be sent and summed in bfloat16 or wider, within the bound.
No kernel may reach another device: no remote copies, remote signals or barrier semaphores. Data moves between devices by JAX's collectives and lax.ppermute only.
A program may use at most 320 MiB of HBM per device.

```python
import jax
import jax.numpy as jnp
from jax import lax

D = 1024
HEADS = 16
HEAD = 64
FF = 4096
LAYERS = 2
SEQ_TOK = 128
MINDOC = 200
MAXDOC = 1500
SEQS = 2
LENGTH = 1024
BATCH = 8


def draw_documents(key, part):
    key = jax.random.fold_in(key, 11)
    doc_count = LENGTH // MINDOC + 2
    length_key, first_key, pick_key = jax.random.split(key, 3)
    doc_lengths = jax.random.randint(length_key, (BATCH, doc_count), MINDOC, MAXDOC + 1)
    opening = jax.random.randint(first_key, (BATCH,), 1, SEQ_TOK)
    chosen = jax.random.randint(pick_key, (BATCH // SEQS,), 0, SEQS)
    row_index = jnp.arange(BATCH)
    chosen_rows = jnp.repeat(chosen, SEQS)
    marked = row_index % SEQS == chosen_rows
    shortest = row_index % SEQS == (chosen_rows + 1) % SEQS
    doc_lengths = jnp.where(shortest[:, None], MINDOC, doc_lengths)
    doc_lengths = doc_lengths.at[:, 0].set(jnp.where(marked, opening, doc_lengths[:, 0]))
    doc_lengths = doc_lengths.at[:, 1].set(jnp.where(marked, LENGTH, doc_lengths[:, 1]))
    doc_ends = jnp.cumsum(doc_lengths, axis=1)
    places = jnp.arange(LENGTH)
    passed = (doc_ends[:, None, :] <= places[None, :, None]).astype(jnp.int32)
    return jnp.sum(passed, axis=2).astype(jnp.int32)


def raised(entries, key, source, target, shards_of, factor):
    owner, partner = [(jnp.arange(entries.shape[dim]) // (entries.shape[dim] // shards_of)).reshape([-1 if axis == dim else 1 for axis in range(entries.ndim)]) for dim in (source, target)]
    chosen = jax.random.permutation(key, shards_of)[partner]
    strong = (owner == chosen) | (owner == (partner + shards_of // 2) % shards_of)
    return jnp.where(strong, factor * entries, entries)


def block_levels(key, dims, cuts, least, top_value):
    loudness = 1.0
    for dim, parts in cuts:
        steps = jax.random.uniform(jax.random.fold_in(jax.random.fold_in(key, 6), dim), (parts,), jnp.float32, least / len(cuts), top_value / len(cuts))
        loudness = loudness * jnp.repeat(jnp.exp(steps), dims[dim] // parts).reshape((-1,) + (1,) * (len(dims) - 1 - dim))
    return loudness


def noise(key, dims, width, bound, shards=(), kind=jnp.bfloat16):
    values = width * jax.random.normal(key, dims, jnp.float32)
    if shards:
        values = values * block_levels(key, dims, shards, -0.22, 0.18)
    return jnp.clip(values, -bound, bound).astype(kind)


def bell_draw_with(rng, dims, width, limit, cuts, heavy, held_as=jnp.bfloat16):
    values = width * jax.random.normal(rng, dims, jnp.float32)
    if cuts:
        values = values * block_levels(rng, dims, cuts, -0.22, 0.18)
    return jnp.clip(raised(values, jax.random.fold_in(rng, 3), *heavy), -limit, limit).astype(held_as)


def setup_inputs(seed: int = 0) -> dict:
    arg_keys = jax.random.split(jax.random.key(seed), 14)
    layer_input = bell_draw_with(arg_keys[0], (BATCH, LENGTH, D), 1.0, 8.0, ((0, 4), (1, 8)), (1, 2, 8, 2.0))
    documents = draw_documents(jax.random.fold_in(arg_keys[13], 71), 0)
    cotangent = noise(arg_keys[2], (BATCH, LENGTH, D), 1.0, 6.0, ((0, 4), (1, 8)))
    attend_weight = noise(arg_keys[3], (LAYERS, 3, D, D), (D // 2) ** -0.5, 0.25, ((2, 32),), jnp.float32)
    attend_bias = noise(arg_keys[4], (LAYERS, 2, D), 0.5, 3.0, ((2, 32),), jnp.float32)
    output_weight = noise(arg_keys[5], (LAYERS, D, D), (D // 8) ** -0.5, 0.5, ((1, 32),), jnp.float32)
    output_bias = noise(arg_keys[6], (LAYERS, D), 0.5, 3.0, ((1, 32),), jnp.float32)
    norm_gain = jnp.clip(1.0 + 0.15 * jax.random.normal(arg_keys[7], (LAYERS, 2, D), jnp.float32), 0.25, 1.75)
    norm_shift = noise(arg_keys[8], (LAYERS, 2, D), 0.3, 1.75, ((2, 32),), jnp.float32)
    expand_weight = noise(arg_keys[9], (LAYERS, D, FF), D ** -0.5, 0.1875, ((1, 32),), jnp.float32)
    expand_bias = noise(arg_keys[10], (LAYERS, FF), 0.5, 3.0, ((1, 32),), jnp.float32)
    reduce_weight = noise(arg_keys[11], (LAYERS, FF, D), FF ** -0.5, 0.09375, ((1, 32),), jnp.float32)
    reduce_bias = noise(arg_keys[12], (LAYERS, D), 0.5, 3.0, ((1, 32),), jnp.float32)
    return dict(layer_input=layer_input, documents=documents, cotangent=cotangent, attend_weight=attend_weight, attend_bias=attend_bias, output_weight=output_weight, output_bias=output_bias, norm_gain=norm_gain, norm_shift=norm_shift, expand_weight=expand_weight, expand_bias=expand_bias, reduce_weight=reduce_weight, reduce_bias=reduce_bias)


@jax.custom_vjp
def low(v):
    return lax.optimization_barrier(v.astype(jnp.bfloat16)).astype(jnp.float32)

@jax.custom_vjp
def low_back(v):
    return v

def low_keep(v):
    return (low(v), None)

def low_pass(kept, grad):
    return (grad,)

def back_keep(v):
    return (v, None)

def back_low(kept, grad):
    return (low(grad),)
low.defvjp(low_keep, low_pass)
low_back.defvjp(back_keep, back_low)
EPSILON = 1e-05
NEG_FILL = -1e+30
HIGHEST = lax.Precision.HIGHEST

def matmul(left_side, right_side):
    return jnp.dot(left_side, right_side, precision=HIGHEST, preferred_element_type=jnp.float32)

def layer_norm(token_rows, gain_row, shift_row):
    mean_row = lax.optimization_barrier(jnp.mean(token_rows, axis=-1, keepdims=True))
    centred = token_rows - mean_row
    variance = lax.optimization_barrier(jnp.mean(centred * centred, axis=-1, keepdims=True))
    return centred * lax.rsqrt(variance + EPSILON) * gain_row + shift_row

def attention(queries, keys_all, values_all, segment_row):
    length = queries.shape[0]
    block_rows = min(512, length)
    block_count = length // block_rows
    key_heads = keys_all.reshape(length, HEADS, HEAD)
    value_heads = values_all.reshape(length, HEADS, HEAD)
    scale_factor = HEAD ** (-0.5)

    def one_block(pieces):
        query_part, segment_part = pieces
        scores = jnp.einsum('qhd,khd->hqk', query_part, key_heads, precision=HIGHEST, preferred_element_type=jnp.float32) * scale_factor
        scores = low_back(scores)
        allowed = segment_part[:, None] == segment_row[None, :]
        scores = jnp.where(allowed[None], scores, NEG_FILL)
        soft_probs = jax.nn.softmax(scores, axis=-1)
        return jnp.einsum('hqk,khd->qhd', low(soft_probs), value_heads, precision=HIGHEST, preferred_element_type=jnp.float32)
    contexts = lax.map(jax.checkpoint(one_block), (queries.reshape(block_count, block_rows, HEADS, HEAD), segment_row.reshape(block_count, block_rows)))
    return contexts.reshape(length, HEADS * HEAD)

def encoder_layer(token_rows, segment_row, weights):
    attend_weight, attend_bias, output_weight, output_bias, norm_gain, norm_shift, expand_weight, expand_bias, reduce_weight, reduce_bias = [low(weight_item) for weight_item in weights]
    rows_low = low(token_rows)
    queries = low_back(low(matmul(rows_low, attend_weight[0]) + attend_bias[0]))
    keys_all = low_back(low(matmul(rows_low, attend_weight[1])))
    values_all = low_back(low(matmul(rows_low, attend_weight[2]) + attend_bias[1]))
    contexts = low_back(low(attention(queries, keys_all, values_all, segment_row)))
    branch = low_back(matmul(contexts, output_weight) + output_bias)
    first_norm = layer_norm(token_rows + branch, norm_gain[0], norm_shift[0])
    expanded = low_back(matmul(low(first_norm), expand_weight) + expand_bias)
    activated = jax.nn.gelu(expanded, approximate=False)
    reduced = low_back(matmul(low(activated), reduce_weight) + reduce_bias)
    return layer_norm(first_norm + reduced, norm_gain[1], norm_shift[1])

def encoder_stack(token_rows, segment_row, params):
    for layer_index in range(LAYERS):
        token_rows = encoder_layer(token_rows, segment_row, tuple((weight_item[layer_index] for weight_item in params)))
    return token_rows

def reference(layer_input, documents, cotangent, attend_weight, attend_bias, output_weight, output_bias, norm_gain, norm_shift, expand_weight, expand_bias, reduce_weight, reduce_bias):
    params = (attend_weight, attend_bias, output_weight, output_bias, norm_gain, norm_shift, expand_weight, expand_bias, reduce_weight, reduce_bias)

    def one_sequence(totals, pieces):
        token_rows, segment_row, grad_rows = pieces

        def forward(rows_in, weights):
            return encoder_stack(rows_in, segment_row, weights)
        outputs, pullback = jax.vjp(forward, token_rows.astype(jnp.float32), params)
        grad_input, grad_params = pullback(grad_rows.astype(jnp.float32))
        totals = jax.tree.map(lambda earlier, update: earlier + update, totals, grad_params)
        return (totals, (outputs.astype(jnp.bfloat16), grad_input))
    zeros_start = jax.tree.map(jnp.zeros_like, params)
    totals, (layer_output, input_gradient) = lax.scan(one_sequence, zeros_start, (layer_input, documents, cotangent))
    return (layer_output, input_gradient, totals[0], totals[1], totals[2], totals[3], totals[4], totals[5], totals[6], totals[7], totals[8], totals[9])
```

```python
import jax
import jax.numpy as jnp
from jax import lax
from jax.sharding import Mesh, PartitionSpec as P

HEAD = 64
WIDE = 1024
SMALL_ROWS = 16
EPSILON = 1e-05
NEG_FILL = -1e30
BF = jnp.bfloat16
F32 = jnp.float32


def shift_perm(count, step):
    return [(i, (i + step) % count) for i in range(count)]


def swap_core(value):
    return lax.ppermute(value, "c", [(0, 1), (1, 0)])


def gather_shift(value, axes, count):
    place = lax.axis_index(axes)
    pieces = [value] + [
        lax.ppermute(value, axes, shift_perm(count, step)) for step in range(1, count)
    ]
    out = jnp.zeros((count,) + value.shape, value.dtype)
    for step, piece in enumerate(pieces):
        out = lax.dynamic_update_index_in_dim(out, piece, (place - step) % count, 0)
    return out


def scatter_shift(value, axes, count, dim=0):
    place = lax.axis_index(axes)

    def piece(step):
        return lax.dynamic_index_in_dim(value, (place + step) % count, dim, keepdims=False)

    got = [lax.ppermute(piece(step), axes, shift_perm(count, step)) for step in range(1, count)]
    total = piece(0).astype(F32)
    for part in got:
        total = total + part.astype(F32)
    return total


def both_cores(value):
    return jnp.concatenate([value, swap_core(value)], axis=0)


def sum_cores(partial):
    half = partial.shape[0] // 2
    return partial[:half] + swap_core(partial[half:].astype(BF)).astype(F32)


def matmul(left, right):
    return jnp.dot(left, right, preferred_element_type=F32)


def matmul_tn(left, right):
    return lax.dot_general(left, right, (((0,), (0,)), ((), ())), preferred_element_type=F32)


def matmul_nt(left, right):
    return lax.dot_general(left, right, (((1,), (1,)), ((), ())), preferred_element_type=F32)


def layer_norm(rows, gain, shift):
    mean = jnp.mean(rows, axis=-1, keepdims=True)
    centred = rows - mean
    variance = jnp.mean(centred * centred, axis=-1, keepdims=True)
    return centred * lax.rsqrt(variance + EPSILON) * gain + shift


def layer_norm_back(grad, rows, gain):
    mean = jnp.mean(rows, axis=-1, keepdims=True)
    centred = rows - mean
    variance = jnp.mean(centred * centred, axis=-1, keepdims=True)
    inverse = lax.rsqrt(variance + EPSILON)
    hat = centred * inverse
    grad_hat = grad * gain
    grad_rows = inverse * (
        grad_hat
        - jnp.mean(grad_hat, axis=-1, keepdims=True)
        - hat * jnp.mean(grad_hat * hat, axis=-1, keepdims=True)
    )
    return grad_rows, jnp.sum(grad * hat, axis=0), jnp.sum(grad, axis=0)


def attend_forward(query, key_value, docs_query, docs_key):
    rows, width = query.shape
    heads = width // HEAD
    query_heads = query.reshape(rows, heads, HEAD)
    key_heads = key_value[:, :width].reshape(-1, heads, HEAD)
    value_heads = key_value[:, width:].reshape(-1, heads, HEAD)
    scores = jnp.einsum("qhd,khd->hqk", query_heads, key_heads, preferred_element_type=F32)
    scores = scores * HEAD ** (-0.5)
    allowed = docs_query[:, None] == docs_key[None, :]
    scores = jnp.where(allowed[None], scores, NEG_FILL)
    top = jnp.max(scores, axis=-1, keepdims=True)
    raised = jnp.exp(scores - top)
    total = jnp.sum(raised, axis=-1, keepdims=True)
    soft = (raised / total).astype(BF)
    context = jnp.einsum("hqk,khd->qhd", soft, value_heads, preferred_element_type=F32)
    return context.astype(BF).reshape(rows, width), (top + jnp.log(total))[..., 0]


def attend_backward(grad, query, key_value, log_total, docs_query, docs_key):
    rows, width = query.shape
    heads = width // HEAD
    scale = HEAD ** (-0.5)
    grad_heads = grad.reshape(rows, heads, HEAD)
    query_heads = query.reshape(rows, heads, HEAD)
    key_heads = key_value[:, :width].reshape(-1, heads, HEAD)
    value_heads = key_value[:, width:].reshape(-1, heads, HEAD)
    scores = jnp.einsum("qhd,khd->hqk", query_heads, key_heads, preferred_element_type=F32)
    allowed = docs_query[:, None] == docs_key[None, :]
    scores = jnp.where(allowed[None], scores * scale, NEG_FILL)
    soft = jnp.exp(scores - log_total[..., None])
    grad_value = jnp.einsum("hqk,qhd->khd", soft.astype(BF), grad_heads, preferred_element_type=F32)
    grad_soft = jnp.einsum("qhd,khd->hqk", grad_heads, value_heads, preferred_element_type=F32)
    low = soft * (grad_soft - jnp.sum(soft * grad_soft, axis=-1, keepdims=True))
    low = low.astype(BF)
    grad_query = jnp.einsum("hqk,khd->qhd", low, key_heads, preferred_element_type=F32) * scale
    grad_key = jnp.einsum("hqk,qhd->khd", low, query_heads, preferred_element_type=F32) * scale
    keys = key_value.shape[0]
    return (
        grad_query.astype(BF).reshape(rows, width),
        grad_key.reshape(keys, width),
        grad_value.reshape(keys, width),
    )


def ffn_forward(rows_low, packed, bias, rows1):
    first = packed[:, :rows1].reshape(WIDE, WIDE)
    second = packed[:, rows1 : 2 * rows1].reshape(WIDE, WIDE)
    reduce = packed[:, 2 * rows1 :].reshape(2 * WIDE, WIDE)
    expanded = jnp.concatenate([matmul(rows_low, first), matmul(rows_low, second)], axis=1) + bias
    active = jax.nn.gelu(expanded, approximate=False).astype(BF)
    return matmul(active, reduce), expanded


def ffn_backward(grad_low, rows_low, expanded, packed, rows1):
    chips = packed.shape[0]
    first = packed[:, :rows1].reshape(WIDE, WIDE)
    second = packed[:, rows1 : 2 * rows1].reshape(WIDE, WIDE)
    reduce = packed[:, 2 * rows1 :].reshape(2 * WIDE, WIDE)
    active, pull = jax.vjp(lambda v: jax.nn.gelu(v, approximate=False), expanded)
    grad_reduce = matmul_tn(active.astype(BF), grad_low).astype(BF)
    grad_expanded = pull(matmul_nt(grad_low, reduce))[0].astype(BF)
    left, right = grad_expanded[:, :WIDE], grad_expanded[:, WIDE:]
    grad_first = matmul_tn(rows_low, left).astype(BF)
    grad_second = matmul_tn(rows_low, right).astype(BF)
    grad_rows = matmul_nt(left, first) + matmul_nt(right, second)
    grads = jnp.concatenate(
        [
            grad_first.reshape(chips, rows1, WIDE),
            grad_second.reshape(chips, rows1, WIDE),
            grad_reduce.reshape(chips, -1, WIDE),
        ],
        axis=1,
    )
    return grads, grad_rows, jnp.sum(grad_expanded, axis=0, dtype=F32)


def make_body(n_fa, n_fb, n_h, n_m):
    n_f, n_z = n_fa * n_fb, n_h * n_m
    n_chip = n_f * n_z
    z_axes = ("h", "m")

    def body(
        layer_input,
        documents,
        cotangent,
        attend_weight,
        attend_bias,
        output_weight,
        output_bias,
        norm_gain,
        norm_shift,
        expand_weight,
        expand_bias,
        reduce_weight,
        reduce_bias,
    ):
        core, half = lax.axis_index("c"), lax.axis_index("h")
        layers = attend_weight.shape[0]
        tokens = layer_input.shape[1]
        rows0 = attend_weight.shape[2]
        rows1 = 2 * rows0
        units = reduce_weight.shape[1]
        width = WIDE // 2
        own_tokens = 2 * tokens

        def by_core(own, other, axis):
            return jnp.where(
                core == 0,
                jnp.concatenate([own, other], axis=axis),
                jnp.concatenate([other, own], axis=axis),
            )

        def to_halves(pair):
            keep = jnp.where(half == 0, pair[0], pair[1])
            give = jnp.where(half == 0, pair[1], pair[0])
            got = lax.ppermute(give, "h", [(0, 1), (1, 0)])
            first = jnp.where(half == 0, keep, got)
            last = jnp.where(half == 0, got, keep)
            return jnp.concatenate([first, last], axis=0)

        def from_halves(rows):
            first, last = rows[:tokens], rows[tokens:]
            keep = jnp.where(half == 0, first, last)
            give = jnp.where(half == 0, last, first)
            got = lax.ppermute(give, "h", [(0, 1), (1, 0)])
            return jnp.where(half == 0, jnp.stack([keep, got]), jnp.stack([got, keep]))

        def smalls_of(layer):
            return jnp.concatenate(
                [
                    attend_bias[layer].reshape(-1),
                    output_bias[layer],
                    norm_gain[layer].reshape(-1),
                    norm_shift[layer].reshape(-1),
                    expand_bias[layer],
                    reduce_bias[layer],
                ]
            )

        small_row = jnp.concatenate([smalls_of(layer) for layer in range(layers)])
        small_len = small_row.shape[0] // layers
        small_row = jnp.pad(small_row.astype(BF), (0, WIDE - layers * small_len))[None]
        small_row = by_core(small_row, swap_core(small_row), 0)
        small_shard = jnp.pad(small_row, ((0, SMALL_ROWS - 2), (0, 0)))

        def shards_of(layer):
            wa = attend_weight[layer].astype(BF)
            wo = output_weight[layer].astype(BF)
            w1 = expand_weight[layer].astype(BF).reshape(rows0, -1, 2, units)
            wa_own = jnp.where(core == 0, wa[..., :width], wa[..., width:])
            wa_give = jnp.where(core == 0, wa[..., width:], wa[..., :width])
            wo_own = jnp.where(core == 0, wo[:, :width], wo[:, width:])
            wo_give = jnp.where(core == 0, wo[:, width:], wo[:, :width])
            w1_own = jnp.where(core == 0, w1[:, :, 0], w1[:, :, 1]).reshape(rows0, 2 * WIDE)
            w1_give = jnp.where(core == 0, w1[:, :, 1], w1[:, :, 0]).reshape(rows0, 2 * WIDE)

            def attn_pack(a, o):
                return jnp.stack(
                    [
                        jnp.concatenate([a[0], a[1]], axis=1),
                        jnp.concatenate([a[2], o], axis=1),
                    ]
                )

            def ffn_pack(w):
                return jnp.stack([w[:, :WIDE], w[:, WIDE:]])

            attn_own, attn_give = attn_pack(wa_own, wo_own), attn_pack(wa_give, wo_give)
            ffn_own, ffn_give = ffn_pack(w1_own), ffn_pack(w1_give)
            got = swap_core(jnp.concatenate([attn_give, ffn_give], axis=0))
            attn = by_core(attn_own, got[:2], 1)
            ffn = by_core(ffn_own, got[2:], 1).reshape(2 * rows1, WIDE)
            ffn = jnp.concatenate([ffn, reduce_weight[layer].astype(BF)], axis=0)
            return attn, ffn

        def gather_attn(attn, extra=None):
            parts = [attn[0], attn[1]]
            if extra is not None:
                parts.append(extra)
            column = gather_shift(jnp.concatenate(parts, axis=0), z_axes, n_z)
            first = column[:, :rows1]
            second = column[:, rows1:]
            first = gather_shift(gather_shift(first, "fb", n_fb), "fa", n_fa)
            second = gather_shift(gather_shift(second, "fa", n_fa), "fb", n_fb)
            second = jnp.swapaxes(second, 0, 1)
            first = first.reshape(n_chip, -1, WIDE)
            second = second.reshape(n_chip, -1, WIDE)
            small = second[:, rows1:]
            query_key = first.reshape(WIDE, WIDE)
            value_out = second[:, :rows1].reshape(WIDE, WIDE)
            out_cols = value_out[:, width:]
            give = jnp.where(core == 0, out_cols[width:], out_cols[:width])
            mine = jnp.where(core == 0, out_cols[:width], out_cols[width:])
            out_rows = by_core(mine, swap_core(give), 1)
            return (query_key, value_out[:, :width], out_rows), small

        def gather_ffn(ffn):
            column = gather_shift(ffn, z_axes, n_z)
            whole = lax.all_gather(column, ("fa", "fb"), axis=0, tiled=True)
            return whole

        attn_w, ffn_w = [], []
        shards = [shards_of(layer) for layer in range(layers)]
        for layer in range(layers):
            if layer == 0:
                got, small = gather_attn(shards[layer][0], small_shard)
            else:
                got, _ = gather_attn(shards[layer][0])
            attn_w.append(got)
            ffn_w.append(gather_ffn(shards[layer][1]))

        small = small[:, :2].reshape(2 * n_chip, WIDE)[:, : layers * small_len].astype(F32)
        small = small.reshape(2 * n_chip, layers, small_len)

        def small_params(layer):
            part = small[:, layer]

            def vector(index):
                return part[:, index * rows0 : (index + 1) * rows0].reshape(-1)

            bias1 = part[:, 7 * rows0 : 7 * rows0 + units].reshape(n_chip, 2, units)
            bias1 = jnp.where(core == 0, bias1[:, 0], bias1[:, 1]).reshape(-1)
            bias2 = part[:, 7 * rows0 + units :].reshape(-1)
            return [vector(index) for index in range(7)] + [bias1, bias2]

        vectors = [small_params(layer) for layer in range(layers)]

        rows_low = to_halves(layer_input)
        docs_own = to_halves(documents)
        docs_chip = both_cores(docs_own)
        docs_all = jnp.concatenate(
            [docs_chip]
            + [lax.ppermute(docs_chip, "m", shift_perm(n_m, step)) for step in range(1, n_m)]
        )
        grad_rows = to_halves(cotangent).astype(F32)

        def core_half(vector):
            return jnp.where(core == 0, vector[:width], vector[width:])

        kept = []
        rows_in = rows_low.astype(F32)
        for layer in range(layers):
            (query_key, value_w, out_w), ffn = attn_w[layer], ffn_w[layer]
            bq, bv, bo, gain0, gain1, shift0, shift1, bias1, bias2 = vectors[layer]
            chip_rows = both_cores(rows_low)
            qk = matmul(chip_rows, query_key)
            query = (qk[:, :width] + core_half(bq)).astype(BF)
            key = qk[:, width:].astype(BF)
            value = (matmul(chip_rows, value_w) + core_half(bv)).astype(BF)
            kv = jnp.concatenate([key, value], axis=1)
            kv = jnp.concatenate(
                [kv]
                + [lax.ppermute(kv, "m", shift_perm(n_m, step)) for step in range(1, n_m)],
                axis=0,
            )
            context, log_total = attend_forward(query, kv, docs_chip, docs_all)
            branch = sum_cores(matmul(context, out_w)) + bo
            first_sum = rows_in + branch
            first_norm = layer_norm(first_sum, gain0, shift0)
            chip_norm = both_cores(first_norm.astype(BF))
            reduced, expanded = ffn_forward(chip_norm, ffn, bias1, rows1)
            second_sum = first_norm + (sum_cores(reduced) + bias2)
            rows_in = layer_norm(second_sum, gain1, shift1)
            kept.append((chip_rows, query, kv, context, log_total, first_sum, chip_norm, expanded, second_sum))
            rows_low = rows_in.astype(BF)
        layer_output = from_halves(rows_low)

        ffn_grads, attn_grads, small_grads = [None] * layers, [None] * layers, [None] * layers
        for layer in reversed(range(layers)):
            chip_rows, query, kv, context, log_total, first_sum, chip_norm, expanded, second_sum = kept[layer]
            (query_key, value_w, out_w), ffn = attn_w[layer], ffn_w[layer]
            gain0, gain1 = vectors[layer][3], vectors[layer][4]
            grad_second, dgain1, dshift1 = layer_norm_back(grad_rows, second_sum, gain1)
            grad_low = grad_second.astype(BF)
            dbias2 = jnp.sum(grad_low, axis=0, dtype=F32)
            packed, grad_norm, dbias1 = ffn_backward(both_cores(grad_low), chip_norm, expanded, ffn, rows1)
            ffn_grads[layer] = packed
            grad_first = grad_second + sum_cores(grad_norm)
            grad_sum, dgain0, dshift0 = layer_norm_back(grad_first, first_sum, gain0)
            grad_low = grad_sum.astype(BF)
            dbo = jnp.sum(grad_low, axis=0, dtype=F32)
            chip_low = both_cores(grad_low)
            grad_context = matmul_nt(chip_low, out_w).astype(BF)
            grad_out = matmul_tn(context, chip_low).astype(BF)
            give = jnp.where(core == 0, grad_out[:, width:], grad_out[:, :width])
            mine = jnp.where(core == 0, grad_out[:, :width], grad_out[:, width:])
            grad_out = by_core(mine, swap_core(give), 0)
            dq, dk, dv = attend_backward(grad_context, query, kv, log_total, docs_chip, docs_all)
            dkv = jnp.concatenate([dk, dv], axis=1)
            chip_tokens = 2 * own_tokens
            total = dkv[:chip_tokens]
            for step in range(1, n_m):
                part = dkv[step * chip_tokens : (step + 1) * chip_tokens].astype(BF)
                total = total + lax.ppermute(part, "m", shift_perm(n_m, -step)).astype(F32)
            dkv = total.astype(BF)
            dk, dv = dkv[:, :width], dkv[:, width:]
            dqk = jnp.concatenate([dq, dk], axis=1)
            grad_qk = matmul_tn(chip_rows, dqk).astype(BF)
            grad_v = matmul_tn(chip_rows, dv).astype(BF)
            attn_grads[layer] = (grad_qk, jnp.concatenate([grad_v, grad_out], axis=1))
            dbq = jnp.sum(dq, axis=0, dtype=F32)
            dbv = jnp.sum(dv, axis=0, dtype=F32)
            grad_rows = grad_sum + sum_cores(matmul_nt(dqk, query_key) + matmul_nt(dv, value_w))

            def spread(vector):
                blank = jnp.zeros_like(vector)
                return by_core(vector, blank, 0)

            dbias1 = dbias1.reshape(n_chip, 1, units)
            dbias1 = by_core(dbias1, jnp.zeros_like(dbias1), 1).reshape(2 * n_chip, units)
            small_grads[layer] = jnp.concatenate(
                [
                    vector.reshape(2 * n_chip, rows0)
                    for vector in (spread(dbq), spread(dbv), dbo, dgain0, dgain1, dshift0, dshift1)
                ]
                + [dbias1, dbias2.reshape(2 * n_chip, rows0)],
                axis=1,
            )
        input_gradient = from_halves(grad_rows)

        small_all = jnp.concatenate(small_grads, axis=1)
        small_all = jnp.pad(small_all, ((0, 0), (0, WIDE - layers * small_len)))
        small_all = small_all.reshape(n_chip, 2, WIDE).astype(BF)
        small_all = jnp.pad(small_all, ((0, 0), (0, SMALL_ROWS - 2), (0, 0)))

        def scatter_attn(first, second, extra=None):
            first = first.reshape(n_fa, n_fb, n_z, rows1, WIDE)
            second = second.reshape(n_chip, rows1, WIDE)
            if extra is not None:
                second = jnp.concatenate([second, extra], axis=1)
            second = second.reshape(n_fa, n_fb, n_z, -1, WIDE)
            first = scatter_shift(first, "fa", n_fa).astype(BF)
            second = scatter_shift(second, "fb", n_fb, 1).astype(BF)
            first = scatter_shift(first, "fb", n_fb)
            second = scatter_shift(second, "fa", n_fa)
            both = jnp.concatenate([first, second], axis=1).astype(BF)
            return scatter_shift(both, z_axes, n_z)

        def core_rows(value, axis):
            count = value.shape[axis] // 2
            low = lax.slice_in_dim(value, 0, count, axis=axis)
            high = lax.slice_in_dim(value, count, 2 * count, axis=axis)
            return jnp.where(core == 0, low, high), jnp.where(core == 0, high, low)

        wa_out, wo_out, w1_out, w2_out = [None] * layers, [None] * layers, [None] * layers, [None] * layers
        for layer in reversed(range(layers)):
            column = lax.psum_scatter(ffn_grads[layer], ("fa", "fb"), scatter_dimension=0, tiled=True)
            mine = scatter_shift(column, z_axes, n_z)
            w2_out[layer] = mine[2 * rows1 :]
            keep, give = core_rows(mine[: 2 * rows1].reshape(2, rows1, WIDE), 1)
            got = swap_core(give)
            keep = jnp.swapaxes(keep, 0, 1).reshape(rows0, -1, 1, units)
            got = jnp.swapaxes(got, 0, 1).reshape(rows0, -1, 1, units)
            w1_out[layer] = by_core(keep, got, 2).reshape(rows0, -1)

            extra = small_all if layer == 0 else None
            mine = scatter_attn(*attn_grads[layer], extra)
            keep, give = core_rows(mine[: 2 * rows1].reshape(2, rows1, 2, width), 1)
            got = swap_core(give)
            full = by_core(keep[:, :, None], got[:, :, None], 2)
            wa_out[layer] = jnp.stack(
                [
                    full[0, :, :, 0].reshape(rows0, WIDE),
                    full[0, :, :, 1].reshape(rows0, WIDE),
                    full[1, :, :, 0].reshape(rows0, WIDE),
                ]
            )
            wo_out[layer] = full[1, :, :, 1].reshape(rows0, WIDE)
            if layer == 0:
                keep, give = core_rows(mine[2 * rows1 : 2 * rows1 + 2], 0)
                row = (keep + swap_core(give))[0, : layers * small_len].reshape(layers, small_len)
        cut = [row[:, index * rows0 : (index + 1) * rows0] for index in range(7)]
        return (
            layer_output,
            input_gradient,
            jnp.stack(wa_out),
            jnp.stack([cut[0], cut[1]], axis=1),
            jnp.stack(wo_out),
            cut[2],
            jnp.stack([cut[3], cut[4]], axis=1),
            jnp.stack([cut[5], cut[6]], axis=1),
            jnp.stack(w1_out),
            row[:, 7 * rows0 : 7 * rows0 + units],
            jnp.stack(w2_out),
            row[:, 7 * rows0 + units :],
        )

    return body


def solution(mesh):
    n_f, n_s = mesh.shape["fsdp"], mesh.shape["seq"]
    sizes = (2, n_f // 2, 2, n_s // 4, 2)
    grid = Mesh(mesh.devices.reshape(sizes), ("fa", "fb", "h", "m", "c"))
    fsdp, seq = ("fa", "fb"), ("h", "m", "c")
    both = fsdp + seq
    tokens = P(fsdp, seq, None)
    third, second = P(None, None, both), P(None, both)
    params = (
        P(None, None, both, None),
        third,
        P(None, both, None),
        second,
        third,
        third,
        P(None, both, None),
        second,
        P(None, both, None),
        second,
    )
    return jax.shard_map(
        make_body(sizes[0], sizes[1], sizes[2], sizes[3]),
        mesh=grid,
        in_specs=(tokens, P(fsdp, seq), tokens) + params,
        out_specs=(tokens, tokens) + params,
        check_vma=False,
    )
```

```python
import jax
import jax.numpy as jnp
from jax import lax
from jax.experimental import pallas as pl
from jax.experimental.pallas import tpu as pltpu
from jax.sharding import Mesh, PartitionSpec as P

HEAD = 64
PAIR = 2 * HEAD
BLOCK = 256
WIDE = 1024
EPSILON = 1e-05
NEG_FILL = -1e30
ROOT_HALF = 0.7071067811865476
ROOT_TWO_PI = 0.3989422804014327
BF = jnp.bfloat16
F32 = jnp.float32
VMEM_BYTES = 56 * 1024 * 1024

def matmul(left, right):
    return jnp.dot(left, right, preferred_element_type=F32)


def matmul_tn(left, right):
    return lax.dot_general(left, right, (((0,), (0,)), ((), ())), preferred_element_type=F32)


def matmul_nt(left, right):
    return lax.dot_general(left, right, (((1,), (1,)), ((), ())), preferred_element_type=F32)


def params(*semantics):
    return pltpu.CompilerParams(dimension_semantics=semantics, vmem_limit_bytes=VMEM_BYTES)


def one_head(value, lane, head):
    mine = lane < HEAD if head == 0 else lane >= HEAD
    return jnp.where(mine, value, jnp.zeros_like(value))


def attend_forward_kernel(q_ref, k_ref, v_ref, col_ref, row_ref, c_ref, log_ref):
    lane = lax.broadcasted_iota(jnp.int32, (BLOCK, PAIR), 1)

    def block(index, carry):
        at = pl.ds(pl.multiple_of(index * BLOCK, BLOCK), BLOCK)
        query = q_ref[at, :]
        allowed = col_ref[at, :] == row_ref[...]
        found, logs = [], []
        for head in (0, 1):
            scores = matmul_nt(one_head(query, lane, head), k_ref[...])
            scores = jnp.where(allowed, scores, NEG_FILL)
            top = jnp.max(scores, axis=1, keepdims=True)
            raised = jnp.exp(scores - top)
            total = jnp.sum(raised, axis=1, keepdims=True)
            found.append(matmul(raised.astype(BF), v_ref[...]) * (1.0 / total))
            logs.append(top + jnp.log(total))
        c_ref[at, :] = jnp.where(lane < HEAD, found[0], found[1]).astype(BF)
        log_ref[:, at] = jnp.where(lane < 1, logs[0], logs[1]).T[:8]
        return carry

    lax.fori_loop(0, q_ref.shape[0] // BLOCK, block, 0)


def pair_specs(tokens):
    return [
        pl.BlockSpec((tokens, PAIR), lambda p: (0, 2 * p)),
        pl.BlockSpec((tokens, PAIR), lambda p: (0, 2 * p + 1)),
        pl.BlockSpec((tokens, PAIR), lambda p: (0, p)),
    ]


def docs_specs(tokens):
    return [
        pl.BlockSpec((tokens, 1), lambda p: (0, 0)),
        pl.BlockSpec((1, tokens), lambda p: (0, 0)),
    ]


def attend_forward(query_key, value, docs):
    tokens, width = value.shape
    pairs = width // PAIR
    return pl.pallas_call(
        attend_forward_kernel,
        grid=(pairs,),
        in_specs=pair_specs(tokens) + docs_specs(tokens),
        out_specs=[
            pl.BlockSpec((tokens, PAIR), lambda p: (0, p)),
            pl.BlockSpec((8, tokens), lambda p: (p, 0)),
        ],
        out_shape=[
            jax.ShapeDtypeStruct((tokens, width), BF),
            jax.ShapeDtypeStruct((8 * pairs, tokens), F32),
        ],
        compiler_params=params("arbitrary"),
        cost_estimate=pl.CostEstimate(
            flops=16 * tokens * tokens * width,
            bytes_accessed=10 * tokens * width,
            transcendentals=tokens * tokens * width // HEAD,
        ),
    )(query_key, query_key, value, docs[:, None], docs[None])


def attend_backward_kernel(
    q_ref, k_ref, v_ref, g_ref, col_ref, row_ref, log_ref, dqk_ref, dv_ref, kt_ref, key_ref, value_ref
):
    lane = lax.broadcasted_iota(jnp.int32, (BLOCK, PAIR), 1)
    down = lax.broadcasted_iota(jnp.int32, (PAIR, BLOCK), 0)
    kt_ref[...] = k_ref[...].T
    key_ref[...] = jnp.zeros_like(key_ref)
    value_ref[...] = jnp.zeros_like(value_ref)

    def block(index, carry):
        at = pl.ds(pl.multiple_of(index * BLOCK, BLOCK), BLOCK)
        query, grad = q_ref[at, :], g_ref[at, :]
        allowed = col_ref[...] == row_ref[:, at]
        found = []
        for head in (0, 1):
            query_one, grad_one = one_head(query, lane, head), one_head(grad, lane, head)
            scores = matmul_nt(k_ref[...], query_one)
            soft = jnp.exp(jnp.where(allowed, scores, NEG_FILL) - log_ref[head : head + 1, at])
            grad_soft = matmul_nt(v_ref[...], grad_one)
            delta = jnp.sum(soft * grad_soft, axis=0, keepdims=True)
            low = (soft * (grad_soft - delta)).astype(BF)
            value_ref[...] += matmul(soft.astype(BF), grad_one)
            key_ref[...] += matmul(low, query_one)
            found.append(matmul(kt_ref[...], low))
        dq = jnp.where(down < HEAD, found[0], found[1]) * HEAD ** (-0.5)
        dqk_ref[at, :PAIR] = dq.T.astype(BF)
        return carry

    lax.fori_loop(0, q_ref.shape[0] // BLOCK, block, 0)
    dqk_ref[:, PAIR:] = key_ref[...].astype(BF)
    dv_ref[...] = value_ref[...].astype(BF)


def attend_backward(grad, query_key, value, logs, docs):
    tokens, width = grad.shape
    pairs = width // PAIR
    return pl.pallas_call(
        attend_backward_kernel,
        grid=(pairs,),
        in_specs=pair_specs(tokens)
        + [pl.BlockSpec((tokens, PAIR), lambda p: (0, p))]
        + docs_specs(tokens)
        + [pl.BlockSpec((8, tokens), lambda p: (p, 0))],
        out_specs=[
            pl.BlockSpec((tokens, 2 * PAIR), lambda p: (0, p)),
            pl.BlockSpec((tokens, PAIR), lambda p: (0, p)),
        ],
        out_shape=[
            jax.ShapeDtypeStruct((tokens, 2 * width), BF),
            jax.ShapeDtypeStruct((tokens, width), BF),
        ],
        scratch_shapes=[
            pltpu.VMEM((PAIR, tokens), BF),
            pltpu.VMEM((tokens, PAIR), F32),
            pltpu.VMEM((tokens, PAIR), F32),
        ],
        compiler_params=params("arbitrary"),
        cost_estimate=pl.CostEstimate(
            flops=40 * tokens * tokens * width,
            bytes_accessed=18 * tokens * width,
            transcendentals=tokens * tokens * width // HEAD,
        ),
    )(query_key, query_key, value, grad, docs[:, None], docs[None], logs)


def join(ref, first, second):
    half = first.shape[0]
    ref[:half, :] = first[...]
    ref[half:, :] = second[...]


def ffn_forward_kernel(
    x0_ref, x1_ref, w1_ref, w2_ref, b_ref, own_ref, give_ref, u_ref, x_ref, total_ref
):
    step = pl.program_id(0)
    tile = b_ref.shape[1]

    @pl.when(step == 0)
    def _():
        join(x_ref, x0_ref, x1_ref)

    expanded = matmul(x_ref[...], w1_ref[...].reshape(WIDE, tile)) + b_ref[...]
    u_ref[...] = expanded
    active = (expanded * (0.5 + 0.5 * lax.erf(expanded * ROOT_HALF))).astype(BF)
    part = matmul(active, w2_ref[...].reshape(tile, WIDE))

    @pl.when(step == 0)
    def _():
        total_ref[...] = part

    @pl.when(step > 0)
    def _():
        total_ref[...] += part

    @pl.when(step == pl.num_programs(0) - 1)
    def _():
        half = own_ref.shape[0]
        own_ref[...] = total_ref[:half, :]
        give_ref[...] = total_ref[half:, :].astype(BF)


def ffn_specs(packed, tile):
    chips, rows = packed.shape[0], packed.shape[1]
    per_half = WIDE // tile
    return [
        pl.BlockSpec((chips, rows // 4, tile), lambda t: (0, t // per_half, t % per_half)),
        pl.BlockSpec((tile * chips // (2 * WIDE), rows // 2, WIDE), lambda t: (t, 1, 0)),
    ]


def ffn_forward(rows_low, packed, bias):
    tokens, tile = 2 * rows_low[0].shape[0], 512
    half = pl.BlockSpec((tokens // 2, WIDE), lambda t: (0, 0))
    return pl.pallas_call(
        ffn_forward_kernel,
        grid=(2 * WIDE // tile,),
        in_specs=[half, half]
        + ffn_specs(packed, tile)
        + [pl.BlockSpec((1, tile), lambda t: (0, t))],
        out_specs=[
            pl.BlockSpec((tokens // 2, WIDE), lambda t: (0, 0)),
            pl.BlockSpec((tokens // 2, WIDE), lambda t: (0, 0)),
            pl.BlockSpec((tokens, tile), lambda t: (0, t)),
        ],
        out_shape=[
            jax.ShapeDtypeStruct((tokens // 2, WIDE), F32),
            jax.ShapeDtypeStruct((tokens // 2, WIDE), BF),
            jax.ShapeDtypeStruct((tokens, 2 * WIDE), F32),
        ],
        scratch_shapes=[pltpu.VMEM((tokens, WIDE), BF), pltpu.VMEM((tokens, WIDE), F32)],
        compiler_params=params("arbitrary"),
        cost_estimate=pl.CostEstimate(
            flops=8 * tokens * WIDE * WIDE,
            bytes_accessed=16 * WIDE * WIDE + 16 * tokens * WIDE,
            transcendentals=2 * tokens * WIDE,
        ),
    )(*rows_low, packed, packed, bias[None])


def ffn_backward_kernel(
    g0_ref,
    g1_ref,
    x0_ref,
    x1_ref,
    u_ref,
    w1_ref,
    w2_ref,
    own_ref,
    give_ref,
    db_ref,
    dw_ref,
    g_ref,
    xt_ref,
    total_ref,
):
    step = pl.program_id(0)
    tile = u_ref.shape[1]
    chips, rows = dw_ref.shape[0], dw_ref.shape[1]
    quarter = rows // 4
    per_half = WIDE // tile
    group = tile * chips // (2 * WIDE)

    @pl.when(step == 0)
    def _():
        join(g_ref, g0_ref, g1_ref)
        half = x0_ref.shape[0]
        xt_ref[:, :half] = x0_ref[...].T
        xt_ref[:, half:] = x1_ref[...].T
        total_ref[...] = jnp.zeros_like(total_ref)

    grad = g_ref[...]
    expanded = u_ref[...]
    normal = 0.5 + 0.5 * lax.erf(expanded * ROOT_HALF)
    active = (expanded * normal).astype(BF)
    slope = normal + expanded * (ROOT_TWO_PI * jnp.exp(-0.5 * expanded * expanded))
    dw2 = matmul_tn(active, grad)
    dw_ref[pl.ds(step * group, group), 2 * quarter :, :] = dw2.astype(BF).reshape(group, 2 * quarter, WIDE)
    low = (matmul_nt(grad, w2_ref[...].reshape(tile, WIDE)) * slope).astype(BF)
    db_ref[...] = jnp.sum(low.astype(F32), axis=0, keepdims=True)
    dw1 = matmul(xt_ref[...], low).astype(BF).reshape(chips, quarter, tile)
    dw_ref[:, pl.ds(pl.multiple_of((step // per_half) * quarter, quarter), quarter),
           pl.ds(pl.multiple_of((step % per_half) * tile, tile), tile)] = dw1
    total_ref[...] += matmul_nt(low, w1_ref[...].reshape(WIDE, tile))

    @pl.when(step == pl.num_programs(0) - 1)
    def _():
        half = own_ref.shape[0]
        own_ref[...] = total_ref[:half, :]
        give_ref[...] = total_ref[half:, :].astype(BF)


def ffn_backward(grad_low, rows_low, expanded, packed):
    tokens, tile = 2 * rows_low[0].shape[0], 256
    half = pl.BlockSpec((tokens // 2, WIDE), lambda t: (0, 0))
    return pl.pallas_call(
        ffn_backward_kernel,
        grid=(2 * WIDE // tile,),
        in_specs=[half] * 4
        + [pl.BlockSpec((tokens, tile), lambda t: (0, t))]
        + ffn_specs(packed, tile),
        out_specs=[
            pl.BlockSpec((tokens // 2, WIDE), lambda t: (0, 0)),
            pl.BlockSpec((tokens // 2, WIDE), lambda t: (0, 0)),
            pl.BlockSpec((1, tile), lambda t: (0, t)),
            pl.BlockSpec(packed.shape, lambda t: (0, 0, 0)),
        ],
        out_shape=[
            jax.ShapeDtypeStruct((tokens // 2, WIDE), F32),
            jax.ShapeDtypeStruct((tokens // 2, WIDE), BF),
            jax.ShapeDtypeStruct((1, 2 * WIDE), F32),
            jax.ShapeDtypeStruct(packed.shape, BF),
        ],
        scratch_shapes=[
            pltpu.VMEM((tokens, WIDE), BF),
            pltpu.VMEM((WIDE, tokens), BF),
            pltpu.VMEM((tokens, WIDE), F32),
        ],
        compiler_params=params("arbitrary"),
        cost_estimate=pl.CostEstimate(
            flops=16 * tokens * WIDE * WIDE,
            bytes_accessed=16 * WIDE * WIDE + 20 * tokens * WIDE,
            transcendentals=4 * tokens * WIDE,
        ),
    )(*grad_low, *rows_low, expanded, packed, packed)


def shift_perm(count, step):
    return [(i, (i + step) % count) for i in range(count)]


def swap_core(value):
    return lax.ppermute(value, "c", [(0, 1), (1, 0)])


def gather_shift(value, axis, count, dim):
    place = lax.axis_index(axis)
    out = jnp.zeros(value.shape[:dim] + (count,) + value.shape[dim:], value.dtype)
    for step in range(count):
        piece = lax.ppermute(value, axis, shift_perm(count, step)) if step else value
        out = lax.dynamic_update_index_in_dim(out, piece, (place - step) % count, dim)
    return out


def scatter_shift(value, axis, count, dim):
    place = lax.axis_index(axis)

    def piece(step):
        return lax.dynamic_index_in_dim(value, (place + step) % count, dim, keepdims=False)

    got = [lax.ppermute(piece(step), axis, shift_perm(count, step)) for step in range(1, count)]
    total = piece(0).astype(F32)
    for part in got:
        total = total + part.astype(F32)
    return total


def together(*values):
    return lax.optimization_barrier(values)


def layer_norm(rows, gain, shift):
    mean = jnp.mean(rows, axis=-1, keepdims=True)
    centred = rows - mean
    variance = jnp.mean(centred * centred, axis=-1, keepdims=True)
    return centred * lax.rsqrt(variance + EPSILON) * gain + shift


def layer_norm_back(grad, rows, gain):
    mean = jnp.mean(rows, axis=-1, keepdims=True)
    centred = rows - mean
    variance = jnp.mean(centred * centred, axis=-1, keepdims=True)
    inverse = lax.rsqrt(variance + EPSILON)
    hat = centred * inverse
    grad_hat = grad * gain
    grad_rows = inverse * (
        grad_hat
        - jnp.mean(grad_hat, axis=-1, keepdims=True)
        - hat * jnp.mean(grad_hat * hat, axis=-1, keepdims=True)
    )
    return grad_rows, jnp.sum(grad * hat, axis=0), jnp.sum(grad, axis=0)


def make_body(n_fa, n_fb, n_h, n_m):
    n_f, n_z = n_fa * n_fb, n_h * n_m
    n_chip, n_s = n_f * n_z, 2 * n_z
    team = 2 * n_m
    width = WIDE // team
    pairs = width // PAIR
    extra = PAIR

    def both_cores(value):
        return jnp.concatenate([value, swap_core(value)], axis=0)

    def team_rows(value):
        parts = [value] + [
            lax.ppermute(value, "m", shift_perm(n_m, step)) for step in range(1, n_m)
        ]
        return [both_cores(part) for part in parts]

    def team_sum(make):
        total = 0.0
        for step in reversed(range(n_m)):
            part = make(step)
            half = part.shape[0] // 2
            part = part[:half] + swap_core(part[half:].astype(BF)).astype(F32)
            if step:
                part = lax.ppermute(part.astype(BF), "m", shift_perm(n_m, -step)).astype(F32)
            total = total + part
        return total

    def pair_up(first, second):
        shape = first.shape[:-1]
        first = first.reshape(shape + (pairs, 1, PAIR))
        second = second.reshape(shape + (pairs, 1, PAIR))
        return jnp.concatenate([first, second], axis=-2).reshape(shape + (2 * width,))

    def body(
        layer_input,
        documents,
        cotangent,
        attend_weight,
        attend_bias,
        output_weight,
        output_bias,
        norm_gain,
        norm_shift,
        expand_weight,
        expand_bias,
        reduce_weight,
        reduce_bias,
    ):
        core, half = lax.axis_index("c"), lax.axis_index("h")
        rank = lax.axis_index(("m", "c"))
        layers = attend_weight.shape[0]
        tokens = layer_input.shape[1]
        rows0 = attend_weight.shape[2]
        rows1 = 2 * rows0
        units = reduce_weight.shape[1]
        lots = units // rows0
        lanes_of = 8 + lots

        def by_core(own, other, axis):
            return jnp.where(
                core == 0,
                jnp.concatenate([own, other], axis=axis),
                jnp.concatenate([other, own], axis=axis),
            )

        def to_halves(pair):
            keep = jnp.where(half == 0, pair[0], pair[1])
            give = jnp.where(half == 0, pair[1], pair[0])
            got = lax.ppermute(give, "h", [(0, 1), (1, 0)])
            first = jnp.where(half == 0, keep, got)
            last = jnp.where(half == 0, got, keep)
            return jnp.concatenate([first, last], axis=0)

        def from_halves(rows):
            first, last = rows[:tokens], rows[tokens:]
            keep = jnp.where(half == 0, first, last)
            give = jnp.where(half == 0, last, first)
            got = lax.ppermute(give, "h", [(0, 1), (1, 0)])
            return jnp.where(half == 0, jnp.stack([keep, got]), jnp.stack([got, keep]))

        def small_lanes(layer):
            return jnp.concatenate(
                [
                    attend_bias[layer],
                    output_bias[layer][None],
                    norm_gain[layer],
                    norm_shift[layer],
                    reduce_bias[layer][None],
                    expand_bias[layer].reshape(lots, rows0),
                ],
                axis=0,
            )

        small = jnp.concatenate([small_lanes(layer) for layer in range(layers)], axis=0)
        small = jnp.pad(small.astype(BF).T, ((0, 0), (0, extra - layers * lanes_of)))

        def attn_shard(layer):
            wa = attend_weight[layer].astype(BF).reshape(3, rows0, team, width)
            wo = output_weight[layer].astype(BF).reshape(rows0, team, width)
            packed = jnp.concatenate([pair_up(wa[0], wa[1]), wa[2], wo], axis=-1)
            packed = jnp.swapaxes(packed, 0, 1)
            if layer == 0:
                more = jnp.broadcast_to(small[None], (team,) + small.shape)
                packed = jnp.concatenate([packed, more], axis=-1)
            return jnp.broadcast_to(packed[None], (n_h,) + packed.shape).reshape((n_s,) + packed.shape[1:])

        def column_attn(shard):
            column = lax.all_to_all(shard, ("h", "m", "c"), 0, 0, tiled=True)
            return column.reshape(n_s * rows0, -1)

        def gather_attn(column):
            first, second = column[:, : 2 * width], column[:, 2 * width :]
            first = gather_shift(gather_shift(first, "fb", n_fb, 0), "fa", n_fa, 0)
            second = gather_shift(gather_shift(second, "fa", n_fa, 0), "fb", n_fb, 1)
            first, second = first.reshape(WIDE, -1), second.reshape(WIDE, -1)
            out = second[:, width : 2 * width].reshape(team, width, width)
            out = lax.all_to_all(out, ("m", "c"), 0, 0, tiled=True)
            out = jnp.swapaxes(out, 0, 1).reshape(width, WIDE)
            return (first, second[:, :width], out), second[:, 2 * width :]

        def ffn_shard(layer):
            w1 = expand_weight[layer].astype(BF).reshape(rows0, -1, 2, units)
            own = jnp.where(core == 0, w1[:, :, 0], w1[:, :, 1]).reshape(rows0, 2, WIDE)
            give = jnp.where(core == 0, w1[:, :, 1], w1[:, :, 0]).reshape(rows0, 2, WIDE)
            own, give = jnp.swapaxes(own, 0, 1), jnp.swapaxes(give, 0, 1)
            w1 = by_core(own, swap_core(give), 1).reshape(2 * rows1, WIDE)
            shard = jnp.concatenate([w1, reduce_weight[layer].astype(BF)], axis=0)
            return shard

        def column_ffn(shard):
            return gather_shift(shard, ("h", "m"), n_z, 0)

        def gather_ffn(column):
            return lax.all_gather(column, ("fa", "fb"), axis=0, tiled=True)

        attn_w, ffn_w = [None] * layers, [None] * layers
        attn_column = column_attn(attn_shard(0))
        rows_low = to_halves(layer_input)
        parts = team_rows(rows_low)
        parts, attn_column, ffn_part = together(parts, attn_column, ffn_shard(0))
        ffn_column = column_ffn(ffn_part)
        attn_w[0], small_all = gather_attn(attn_column)

        small_all = small_all.T.astype(F32)

        def small_params(layer):
            part = small_all[layer * lanes_of : (layer + 1) * lanes_of]
            bias1 = jnp.swapaxes(part[8:].reshape(lots, n_chip, 2, rows0), 0, 1)
            bias1 = jnp.swapaxes(bias1, 1, 2)
            bias1 = jnp.where(core == 0, bias1[:, 0], bias1[:, 1]).reshape(-1)
            return [part[index] for index in range(8)] + [bias1]

        vectors = [small_params(layer) for layer in range(layers)]

        def own_width(vector):
            return lax.dynamic_slice_in_dim(vector, rank * width, width)

        docs = jnp.concatenate(team_rows(to_halves(documents)))
        scale = pair_up(jnp.full((width,), HEAD ** (-0.5), F32), jnp.ones((width,), F32))

        kept = []
        rows_in = rows_low.astype(F32)
        for layer in range(layers):
            qk_w, v_w, out_w = attn_w[layer]
            bq, bv, bo, gain0, gain1, shift0, shift1, bias2, bias1 = vectors[layer]
            bias_qk = pair_up(own_width(bq), jnp.zeros((width,), F32))
            bias_v = own_width(bv)
            if layer:
                parts = team_rows(rows_low)
            qk = jnp.concatenate([((matmul(p, qk_w) + bias_qk) * scale).astype(BF) for p in parts])
            value = jnp.concatenate([(matmul(p, v_w) + bias_v).astype(BF) for p in parts])
            if layer == 0:
                qk, value, ffn_column = together(qk, value, ffn_column)
                ffn_w[0] = gather_ffn(ffn_column)
                qk, out_w, attn_part, ffn_part, cotangent = together(
                    qk, out_w, attn_shard(1), ffn_shard(1), cotangent
                )
                attn_w[1] = gather_attn(column_attn(attn_part))[0]
                ffn_column = column_ffn(ffn_part)
                grad_rows = to_halves(cotangent).astype(F32)
            context, logs = attend_forward(qk, value, docs)
            chip_rows = parts[0].shape[0]
            first_sum = rows_in + bo + team_sum(
                lambda step: matmul(context[step * chip_rows : (step + 1) * chip_rows], out_w)
            )
            first_norm = layer_norm(first_sum, gain0, shift0)
            norm_low = first_norm.astype(BF)
            chip_norm = (norm_low, swap_core(norm_low))
            if layer == 0:
                chip_norm, attn_w[1], ffn_column = together(chip_norm, attn_w[1], ffn_column)
                ffn_w[1] = gather_ffn(ffn_column)
            reduced, give, expanded = ffn_forward(chip_norm, ffn_w[layer], bias1)
            second_sum = first_norm + (reduced + swap_core(give).astype(F32) + bias2)
            rows_in = layer_norm(second_sum, gain1, shift1)
            kept.append((parts, qk, value, context, logs, first_sum, chip_norm, expanded, second_sum))
            rows_low = rows_in.astype(BF)
        layer_output = from_halves(rows_low)

        def own_ffn(mine):
            w1 = mine[:, : 2 * rows1].reshape(layers, 2, rows1, WIDE)
            keep = jnp.where(core == 0, w1[:, :, :rows0], w1[:, :, rows0:])
            give = jnp.where(core == 0, w1[:, :, rows0:], w1[:, :, :rows0])
            got = swap_core(give)
            keep = jnp.swapaxes(keep, 1, 2).reshape(layers, rows0, -1, 1, units)
            got = jnp.swapaxes(got, 1, 2).reshape(layers, rows0, -1, 1, units)
            return by_core(keep, got, 3).reshape(layers, rows0, -1), mine[:, 2 * rows1 :]

        def scatter_attn(first, second):
            first = first.reshape(n_fa, n_fb, n_s * rows0, -1)
            second = second.reshape(n_fa, n_fb, n_s * rows0, -1)
            first = scatter_shift(first, "fa", n_fa, 0).astype(BF)
            second = scatter_shift(second, "fb", n_fb, 1).astype(BF)
            return first, second

        def finish_attn(first, second):
            first = scatter_shift(first, "fb", n_fb, 0)
            second = scatter_shift(second, "fa", n_fa, 0)
            column = jnp.concatenate([first, second], axis=1).astype(BF)
            return column.reshape(n_s, rows0, -1)

        def own_attn(columns):
            column = jnp.concatenate(columns, axis=-1)
            pieces = lax.all_to_all(column, ("h", "m", "c"), 0, 0, tiled=True)
            pieces = jnp.sum(pieces.reshape((n_h, team, rows0, -1)).astype(F32), axis=0)
            fours = pieces[..., : 4 * width * layers].reshape(team, rows0, layers, 4 * width)
            qk = fours[..., : 2 * width].reshape(team, rows0, layers, pairs, 2, PAIR)
            query = qk[..., 0, :].reshape(team, rows0, layers, width)
            key = qk[..., 1, :].reshape(team, rows0, layers, width)
            value, out = fours[..., 2 * width : 3 * width], fours[..., 3 * width :]

            def whole(four):
                return jnp.transpose(four, (2, 1, 0, 3)).reshape(layers, rows0, WIDE)

            wa = jnp.stack([whole(query), whole(key), whole(value)], axis=1)
            return wa, whole(out), jnp.sum(pieces[..., 4 * width * layers :], axis=0)

        attn_columns, ffn_mine = [None] * layers, [None] * layers
        small_grads = [None] * layers
        for layer in reversed(range(layers)):
            parts, qk, value, context, logs, first_sum, chip_norm, expanded, second_sum = kept[layer]
            (qk_w, v_w, out_w), ffn = attn_w[layer], ffn_w[layer]
            gain0, gain1 = vectors[layer][3], vectors[layer][4]
            grad_second, dgain1, dshift1 = layer_norm_back(grad_rows, second_sum, gain1)
            grad_low = grad_second.astype(BF)
            dbias2 = jnp.sum(grad_low, axis=0, dtype=F32)
            chip_low = (grad_low, swap_core(grad_low))
            if layer + 1 < layers:
                chip_low, attn_half = together(chip_low, attn_half)
            reduced, give, dbias1, packed = ffn_backward(chip_low, chip_norm, expanded, ffn)
            if layer + 1 < layers:
                attn_columns[layer + 1] = finish_attn(*attn_half)
                ffn_last = ffn_column
            ffn_column = lax.psum_scatter(packed, ("fa", "fb"), scatter_dimension=0, tiled=True)
            grad_first = grad_second + (reduced + swap_core(give).astype(F32))
            grad_sum, dgain0, dshift0 = layer_norm_back(grad_first, first_sum, gain0)
            grad_low = grad_sum.astype(BF)
            dbo = jnp.sum(grad_low, axis=0, dtype=F32)
            grads = team_rows(grad_low)
            if layer + 1 < layers:
                grads, ffn_last = together(grads, ffn_last)
                ffn_mine[layer + 1] = scatter_shift(ffn_last, ("h", "m"), n_z, 0)
            grad_context = jnp.concatenate([matmul_nt(g, out_w).astype(BF) for g in grads])
            chip_rows = grads[0].shape[0]

            def piece(rows, step):
                return rows[step * chip_rows : (step + 1) * chip_rows]

            grad_out = sum(matmul_tn(piece(context, step), g) for step, g in enumerate(grads))
            grad_out = jnp.swapaxes(grad_out.astype(BF).reshape(width, team, width), 0, 1)
            grad_out = lax.all_to_all(grad_out, ("m", "c"), 0, 0, tiled=True).reshape(WIDE, width)
            if layer + 1 == layers:
                grad_context, layer_output = together(grad_context, layer_output)
            dqk, dv = attend_backward(grad_context, qk, value, logs, docs)
            if layer + 1 < layers:
                dqk, ffn_mine[layer + 1], attn_columns[layer + 1] = together(
                    dqk, ffn_mine[layer + 1], attn_columns[layer + 1]
                )
            grad_qk = sum(matmul_tn(p, piece(dqk, step)) for step, p in enumerate(parts)).astype(BF)
            grad_v = sum(matmul_tn(p, piece(dv, step)) for step, p in enumerate(parts)).astype(BF)
            dqk, dv, grad_qk, grad_v = together(dqk, dv, grad_qk, grad_v)
            grad_rows = grad_sum + team_sum(
                lambda step: matmul_nt(piece(dqk, step), qk_w) + matmul_nt(piece(dv, step), v_w)
            )
            dbq = jnp.sum(dqk.reshape(-1, pairs, 2, PAIR)[:, :, 0], axis=0, dtype=F32)
            dbv = jnp.sum(dv, axis=0, dtype=F32)

            def spread(vector):
                blank = jnp.zeros((WIDE,), F32)
                return lax.dynamic_update_slice_in_dim(blank, vector.reshape(-1), rank * width, 0)

            dbias1 = dbias1.reshape(n_chip, 1, lots, rows0)
            dbias1 = by_core(dbias1, jnp.zeros_like(dbias1), 1).reshape(2 * n_chip, lots, rows0)
            dbias1 = jnp.swapaxes(dbias1, 0, 1).reshape(lots, WIDE)
            small_grads[layer] = jnp.concatenate(
                [
                    jnp.stack(
                        [spread(dbq), spread(dbv), dbo, dgain0, dgain1, dshift0, dshift1, dbias2]
                    ),
                    dbias1,
                ]
            )
            second = [grad_v, grad_out]
            if layer == 0:
                lanes = jnp.concatenate(small_grads, axis=0).T.astype(BF)
                second.append(jnp.pad(lanes, ((0, 0), (0, extra - layers * lanes_of))))
            attn_half = scatter_attn(grad_qk, jnp.concatenate(second, axis=1))
        ffn_mine[0] = scatter_shift(ffn_column, ("h", "m"), n_z, 0)
        attn_columns[0] = finish_attn(*attn_half)
        attn_columns[0], ffn_mine[0] = together(attn_columns[0], ffn_mine[0])
        wa_out, wo_out, more = own_attn(attn_columns[::-1])
        w1_out, w2_out = own_ffn(jnp.stack(ffn_mine))
        input_gradient = from_halves(grad_rows.astype(BF)).astype(F32)

        more = more[:, : layers * lanes_of].T.reshape(layers, lanes_of, rows0)
        return (
            layer_output,
            input_gradient,
            wa_out[::-1],
            more[:, :2],
            wo_out[::-1],
            more[:, 2],
            more[:, 3:5],
            more[:, 5:7],
            w1_out,
            more[:, 8:].reshape(layers, units),
            w2_out,
            more[:, 7],
        )

    return body


def solution(mesh):
    n_f, n_s = mesh.shape["fsdp"], mesh.shape["seq"]
    sizes = (2, n_f // 2, 2, n_s // 4, 2)
    grid = Mesh(mesh.devices.reshape(sizes), ("fa", "fb", "h", "m", "c"))
    fsdp, seq = ("fa", "fb"), ("h", "m", "c")
    both = fsdp + seq
    tokens = P(fsdp, seq, None)
    third, second = P(None, None, both), P(None, both)
    weights = (
        P(None, None, both, None),
        third,
        P(None, both, None),
        second,
        third,
        third,
        P(None, both, None),
        second,
        P(None, both, None),
        second,
    )
    return jax.shard_map(
        make_body(*sizes[:4]),
        mesh=grid,
        in_specs=(tokens, P(fsdp, seq), tokens) + weights,
        out_specs=(tokens, tokens) + weights,
        check_vma=False,
    )
```

```python
import jax
import jax.numpy as jnp
from jax import lax
from jax.experimental import pallas as pl
from jax.experimental.pallas import tpu as pltpu
from jax.sharding import Mesh, PartitionSpec as P

HEAD = 64
PAIR = 2 * HEAD
BLOCK = 256
SUB = 256
FFN_TILE = 512
FFN_BACK_TILE = 512
WIDE = 1024
EPSILON = 1e-05
NEG_FILL = -1e30
ROOT_HALF = 0.7071067811865476
ROOT_TWO_PI = 0.3989422804014327
BF = jnp.bfloat16
F32 = jnp.float32
VMEM_BYTES = 56 * 1024 * 1024

def matmul(left, right):
    return jnp.dot(left, right, preferred_element_type=F32)


def matmul_tn(left, right):
    return lax.dot_general(left, right, (((0,), (0,)), ((), ())), preferred_element_type=F32)


def matmul_nt(left, right):
    return lax.dot_general(left, right, (((1,), (1,)), ((), ())), preferred_element_type=F32)


def params(*semantics):
    return pltpu.CompilerParams(dimension_semantics=semantics or None, vmem_limit_bytes=VMEM_BYTES)


def one_head(value, lane, head):
    mine = lane < HEAD if head == 0 else lane >= HEAD
    return jnp.where(mine, value, jnp.zeros_like(value))


def attend_forward_kernel(q_ref, k_ref, v_ref, col_ref, row_ref, c_ref, log_ref):
    lane = lax.broadcasted_iota(jnp.int32, (BLOCK, PAIR), 1)

    def block(index, carry):
        at = pl.ds(pl.multiple_of(index * BLOCK, BLOCK), BLOCK)
        query = q_ref[at, :]
        allowed = col_ref[at, :] == row_ref[...]
        found, logs = [], []
        for head in (0, 1):
            scores = matmul_nt(one_head(query, lane, head), k_ref[...])
            scores = jnp.where(allowed, scores, NEG_FILL)
            top = jnp.max(scores, axis=1, keepdims=True)
            raised = jnp.exp(scores - top)
            total = jnp.sum(raised, axis=1, keepdims=True)
            found.append(matmul(raised.astype(BF), v_ref[...]) * (1.0 / total))
            logs.append(top + jnp.log(total))
        c_ref[at, :] = jnp.where(lane < HEAD, found[0], found[1]).astype(BF)
        log_ref[:, at] = jnp.where(lane < 1, logs[0], logs[1]).T[:8]
        return carry

    lax.fori_loop(0, q_ref.shape[0] // BLOCK, block, 0)


def pair_specs(tokens):
    return [
        pl.BlockSpec((tokens, PAIR), lambda p: (0, 2 * p)),
        pl.BlockSpec((tokens, PAIR), lambda p: (0, 2 * p + 1)),
        pl.BlockSpec((tokens, PAIR), lambda p: (0, p)),
    ]


def docs_specs(tokens):
    return [
        pl.BlockSpec((tokens, 1), lambda p: (0, 0)),
        pl.BlockSpec((1, tokens), lambda p: (0, 0)),
    ]


def attend_forward(query_key, value, docs):
    tokens, width = value.shape
    pairs = width // PAIR
    return pl.pallas_call(
        attend_forward_kernel,
        grid=(pairs,),
        in_specs=pair_specs(tokens) + docs_specs(tokens),
        out_specs=[
            pl.BlockSpec((tokens, PAIR), lambda p: (0, p)),
            pl.BlockSpec((8, tokens), lambda p: (p, 0)),
        ],
        out_shape=[
            jax.ShapeDtypeStruct((tokens, width), BF),
            jax.ShapeDtypeStruct((8 * pairs, tokens), F32),
        ],
        compiler_params=params("arbitrary"),
        cost_estimate=pl.CostEstimate(
            flops=16 * tokens * tokens * width,
            bytes_accessed=10 * tokens * width,
            transcendentals=tokens * tokens * width // HEAD,
        ),
    )(query_key, query_key, value, docs[:, None], docs[None])


def attend_backward_kernel(
    q_ref, k_ref, v_ref, g_ref, col_ref, row_ref, log_ref, dqk_ref, dv_ref, kt_ref, key_ref, value_ref
):
    lane = lax.broadcasted_iota(jnp.int32, (BLOCK, PAIR), 1)
    down = lax.broadcasted_iota(jnp.int32, (PAIR, BLOCK), 0)
    kt_ref[...] = k_ref[...].T
    key_ref[...] = jnp.zeros_like(key_ref)
    value_ref[...] = jnp.zeros_like(value_ref)

    def block(index, carry):
        at = pl.ds(pl.multiple_of(index * BLOCK, BLOCK), BLOCK)
        query, grad = q_ref[at, :], g_ref[at, :]
        allowed = col_ref[...] == row_ref[:, at]
        found = []
        for head in (0, 1):
            query_one, grad_one = one_head(query, lane, head), one_head(grad, lane, head)
            scores = matmul_nt(k_ref[...], query_one)
            soft = jnp.exp(jnp.where(allowed, scores, NEG_FILL) - log_ref[head : head + 1, at])
            grad_soft = matmul_nt(v_ref[...], grad_one)
            delta = jnp.sum(soft * grad_soft, axis=0, keepdims=True)
            low = (soft * (grad_soft - delta)).astype(BF)
            value_ref[...] += matmul(soft.astype(BF), grad_one)
            key_ref[...] += matmul(low, query_one)
            found.append(matmul(kt_ref[...], low))
        dq = jnp.where(down < HEAD, found[0], found[1]) * HEAD ** (-0.5)
        dqk_ref[at, :PAIR] = dq.T.astype(BF)
        return carry

    lax.fori_loop(0, q_ref.shape[0] // BLOCK, block, 0)
    dqk_ref[:, PAIR:] = key_ref[...].astype(BF)
    dv_ref[...] = value_ref[...].astype(BF)


def attend_backward(grad, query_key, value, logs, docs):
    tokens, width = grad.shape
    pairs = width // PAIR
    return pl.pallas_call(
        attend_backward_kernel,
        grid=(pairs,),
        in_specs=pair_specs(tokens)
        + [pl.BlockSpec((tokens, PAIR), lambda p: (0, p))]
        + docs_specs(tokens)
        + [pl.BlockSpec((8, tokens), lambda p: (p, 0))],
        out_specs=[
            pl.BlockSpec((tokens, 2 * PAIR), lambda p: (0, p)),
            pl.BlockSpec((tokens, PAIR), lambda p: (0, p)),
        ],
        out_shape=[
            jax.ShapeDtypeStruct((tokens, 2 * width), BF),
            jax.ShapeDtypeStruct((tokens, width), BF),
        ],
        scratch_shapes=[
            pltpu.VMEM((PAIR, tokens), BF),
            pltpu.VMEM((tokens, PAIR), F32),
            pltpu.VMEM((tokens, PAIR), F32),
        ],
        compiler_params=params("arbitrary"),
        cost_estimate=pl.CostEstimate(
            flops=40 * tokens * tokens * width,
            bytes_accessed=18 * tokens * width,
            transcendentals=tokens * tokens * width // HEAD,
        ),
    )(query_key, query_key, value, grad, docs[:, None], docs[None], logs)


def ffn_forward_kernel(
    x0_ref, x1_ref, w1_ref, w2_ref, b_ref, own_ref, give_ref, gt_ref, slope_ref, xt_ref, x_ref, total_ref
):
    step = pl.program_id(0)
    tile = b_ref.shape[1]

    @pl.when(step == 0)
    def _():
        half = x0_ref.shape[0]
        x_ref[:half, :] = x0_ref[...]
        x_ref[half:, :] = x1_ref[...]
        xt_ref[...] = x_ref[...].T
        total_ref[...] = jnp.zeros_like(total_ref)

    part = 0.0
    for first in range(0, tile, SUB):
        lanes = slice(first, first + SUB)
        group = w2_ref.shape[0] * SUB // tile
        chips = slice(first * w2_ref.shape[0] // tile, first * w2_ref.shape[0] // tile + group)
        expanded = matmul(x_ref[...], w1_ref[:, :, lanes].reshape(WIDE, SUB)) + b_ref[:, lanes]
        normal = 0.5 + 0.5 * lax.erf(expanded * ROOT_HALF)
        slope_ref[:, lanes] = normal + expanded * (ROOT_TWO_PI * jnp.exp(-0.5 * expanded * expanded))
        active = (expanded * normal).astype(BF)
        gt_ref[lanes, :] = active.T
        part = part + matmul(active, w2_ref[chips].reshape(SUB, WIDE))
    total_ref[...] += part

    @pl.when(step == pl.num_programs(0) - 1)
    def _():
        half = own_ref.shape[0]
        own_ref[...] = total_ref[:half, :]
        give_ref[...] = total_ref[half:, :].astype(BF)


def ffn_specs(weights, tile):
    chips = weights[0].shape[0]
    rows = (2 * WIDE) // chips
    per_half = WIDE // tile
    place = weights[1].shape[1] // rows - 1
    return [
        pl.BlockSpec((chips, rows // 2, tile), lambda t: (0, t // per_half, t % per_half)),
        pl.BlockSpec((tile // rows, rows, WIDE), lambda t: (t, place, 0)),
    ]


def ffn_forward(rows_low, weights, bias):
    tokens, tile = 2 * rows_low[0].shape[0], FFN_TILE
    half = pl.BlockSpec((tokens // 2, WIDE), lambda t: (0, 0))
    return pl.pallas_call(
        ffn_forward_kernel,
        grid=(2 * WIDE // tile,),
        in_specs=[half, half]
        + ffn_specs(weights, tile)
        + [pl.BlockSpec((1, tile), lambda t: (0, t))],
        out_specs=[
            half,
            half,
            pl.BlockSpec((tile, tokens), lambda t: (t, 0)),
            pl.BlockSpec((tokens, tile), lambda t: (0, t)),
            pl.BlockSpec((WIDE, tokens), lambda t: (0, 0)),
        ],
        out_shape=[
            jax.ShapeDtypeStruct((tokens // 2, WIDE), F32),
            jax.ShapeDtypeStruct((tokens // 2, WIDE), BF),
            jax.ShapeDtypeStruct((2 * WIDE, tokens), BF),
            jax.ShapeDtypeStruct((tokens, 2 * WIDE), F32),
            jax.ShapeDtypeStruct((WIDE, tokens), BF),
        ],
        scratch_shapes=[pltpu.VMEM((tokens, WIDE), BF), pltpu.VMEM((tokens, WIDE), F32)],
        compiler_params=params("arbitrary"),
        cost_estimate=pl.CostEstimate(
            flops=8 * tokens * WIDE * WIDE,
            bytes_accessed=16 * WIDE * WIDE + 16 * tokens * WIDE,
            transcendentals=4 * tokens * WIDE,
        ),
    )(*rows_low, *weights, bias[None])


def ffn_backward_kernel(
    g0_ref,
    g1_ref,
    xt_ref,
    gt_ref,
    slope_ref,
    w1_ref,
    w2_ref,
    own_ref,
    give_ref,
    db_ref,
    dw1_ref,
    dw2_ref,
    g_ref,
    total_ref,
):
    step = pl.program_id(0)
    tile = slope_ref.shape[1]

    @pl.when(step == 0)
    def _():
        half = g0_ref.shape[0]
        g_ref[:half, :] = g0_ref[...]
        g_ref[half:, :] = g1_ref[...]
        total_ref[...] = jnp.zeros_like(total_ref)

    grad = g_ref[...]
    low = (matmul_nt(grad, w2_ref[...].reshape(tile, WIDE)) * slope_ref[...]).astype(BF)
    dw2_ref[...] = matmul(gt_ref[...], grad).astype(BF).reshape(dw2_ref.shape)
    db_ref[...] = jnp.sum(low.astype(F32), axis=0, keepdims=True)
    dw1_ref[...] = matmul(xt_ref[...], low).astype(BF).reshape(dw1_ref.shape)
    total_ref[...] += matmul_nt(low, w1_ref[...].reshape(WIDE, tile))

    @pl.when(step == pl.num_programs(0) - 1)
    def _():
        half = own_ref.shape[0]
        own_ref[...] = total_ref[:half, :]
        give_ref[...] = total_ref[half:, :].astype(BF)


def ffn_backward(grad_low, saved, weights):
    tokens, tile = 2 * grad_low[0].shape[0], FFN_BACK_TILE
    half = pl.BlockSpec((tokens // 2, WIDE), lambda t: (0, 0))
    active_t, slope, rows_t = saved
    chips = weights[0].shape[0]
    matrix = (chips, 2 * WIDE // chips, WIDE)
    return pl.pallas_call(
        ffn_backward_kernel,
        grid=(2 * WIDE // tile,),
        in_specs=[
            half,
            half,
            pl.BlockSpec((WIDE, tokens), lambda t: (0, 0)),
            pl.BlockSpec((tile, tokens), lambda t: (t, 0)),
            pl.BlockSpec((tokens, tile), lambda t: (0, t)),
        ]
        + ffn_specs(weights, tile),
        out_specs=[
            half,
            half,
            pl.BlockSpec((1, tile), lambda t: (0, t)),
        ]
        + ffn_specs((jax.ShapeDtypeStruct(matrix, BF),) * 2, tile),
        out_shape=[
            jax.ShapeDtypeStruct((tokens // 2, WIDE), F32),
            jax.ShapeDtypeStruct((tokens // 2, WIDE), BF),
            jax.ShapeDtypeStruct((1, 2 * WIDE), F32),
            jax.ShapeDtypeStruct(matrix, BF),
            jax.ShapeDtypeStruct(matrix, BF),
        ],
        scratch_shapes=[pltpu.VMEM((tokens, WIDE), BF), pltpu.VMEM((tokens, WIDE), F32)],
        compiler_params=params("arbitrary"),
        cost_estimate=pl.CostEstimate(
            flops=16 * tokens * WIDE * WIDE,
            bytes_accessed=32 * WIDE * WIDE + 20 * tokens * WIDE,
            transcendentals=0,
        ),
    )(*grad_low, rows_t, active_t, slope, *weights)


def project_forward_kernel(*refs):
    *x_refs, qk_ref, v_ref, bqk_ref, scale_ref, bv_ref, qk_out, v_out = refs
    for index, x_ref in enumerate(x_refs):
        rows = x_ref[...]
        at = slice(index * rows.shape[0], (index + 1) * rows.shape[0])
        qk_out[at, :] = ((matmul(rows, qk_ref[...]) + bqk_ref[...]) * scale_ref[...]).astype(BF)
        v_out[at, :] = (matmul(rows, v_ref[...]) + bv_ref[...]).astype(BF)


def project_forward(pieces, qk_w, v_w, bias_qk, scale, bias_v):
    tokens, width = len(pieces) * pieces[0].shape[0], v_w.shape[1]
    return pl.pallas_call(
        project_forward_kernel,
        out_shape=[
            jax.ShapeDtypeStruct((tokens, 2 * width), BF),
            jax.ShapeDtypeStruct((tokens, width), BF),
        ],
        compiler_params=params(),
        cost_estimate=pl.CostEstimate(
            flops=6 * tokens * WIDE * width,
            bytes_accessed=2 * tokens * (WIDE + 3 * width) + 6 * WIDE * width,
            transcendentals=0,
        ),
    )(*pieces, qk_w, v_w, bias_qk[None], scale[None], bias_v[None])


def project_backward_kernel(*refs):
    *x_refs, dqk_ref, dv_ref, qk_ref, v_ref, gqk_ref, gv_ref, own_ref, give_ref, xt_ref = refs
    rows = x_refs[0].shape[0]
    for index, x_ref in enumerate(x_refs):
        at = slice(index * rows, (index + 1) * rows)
        xt_ref[:, at] = x_ref[...].T
        found = matmul_nt(dqk_ref[at, :], qk_ref[...]) + matmul_nt(dv_ref[at, :], v_ref[...])
        if index % 2 == 0:
            own_ref[index // 2] = found
        else:
            give_ref[index // 2] = found.astype(BF)
    gqk_ref[...] = matmul(xt_ref[...], dqk_ref[...]).astype(BF)
    gv_ref[...] = matmul(xt_ref[...], dv_ref[...]).astype(BF)


def project_backward(pieces, dqk, dv, qk_w, v_w):
    count, rows, width = len(pieces), pieces[0].shape[0], dv.shape[1]
    return pl.pallas_call(
        project_backward_kernel,
        out_shape=[
            jax.ShapeDtypeStruct((WIDE, 2 * width), BF),
            jax.ShapeDtypeStruct((WIDE, width), BF),
            jax.ShapeDtypeStruct((count // 2, rows, WIDE), F32),
            jax.ShapeDtypeStruct((count // 2, rows, WIDE), BF),
        ],
        scratch_shapes=[pltpu.VMEM((WIDE, count * rows), BF)],
        compiler_params=params(),
        cost_estimate=pl.CostEstimate(
            flops=12 * count * rows * WIDE * width,
            bytes_accessed=8 * count * rows * WIDE + 12 * WIDE * width,
            transcendentals=0,
        ),
    )(*pieces, dqk, dv, qk_w, v_w)


def output_backward_kernel(*refs):
    *g_refs, context_ref, out_ref, gcontext_ref, gout_ref = refs
    rows = g_refs[0].shape[0]
    total = 0.0
    for index, g_ref in enumerate(g_refs):
        at = slice(index * rows, (index + 1) * rows)
        gcontext_ref[at, :] = matmul_nt(g_ref[...], out_ref[...]).astype(BF)
        total = total + matmul(context_ref[at, :].T, g_ref[...])
    gout_ref[...] = total.astype(BF)


def output_backward(grads, context, out_w):
    return pl.pallas_call(
        output_backward_kernel,
        out_shape=[
            jax.ShapeDtypeStruct(context.shape, BF),
            jax.ShapeDtypeStruct(out_w.shape, BF),
        ],
        compiler_params=params(),
        cost_estimate=pl.CostEstimate(
            flops=4 * context.shape[0] * context.shape[1] * WIDE,
            bytes_accessed=2 * context.shape[0] * WIDE + 8 * context.shape[1] * WIDE,
            transcendentals=0,
        ),
    )(*grads, context, out_w)


def shift_perm(count, step):
    return [(i, (i + step) % count) for i in range(count)]


def swap_core(value):
    return lax.ppermute(value, "c", [(0, 1), (1, 0)])


def gather_shift(value, axis, count, dim):
    place = lax.axis_index(axis)
    out = jnp.zeros(value.shape[:dim] + (count,) + value.shape[dim:], value.dtype)
    for step in range(count):
        piece = lax.ppermute(value, axis, shift_perm(count, step)) if step else value
        out = lax.dynamic_update_index_in_dim(out, piece, (place - step) % count, dim)
    return out


def scatter_shift(value, axis, count, dim):
    place = lax.axis_index(axis)

    def piece(step):
        return lax.dynamic_index_in_dim(value, (place + step) % count, dim, keepdims=False)

    got = [lax.ppermute(piece(step), axis, shift_perm(count, step)) for step in range(1, count)]
    total = piece(0).astype(F32)
    for part in got:
        total = total + part.astype(F32)
    return total


def together(*values):
    return lax.optimization_barrier(values)


def layer_norm(rows, gain, shift):
    mean = jnp.mean(rows, axis=-1, keepdims=True)
    centred = rows - mean
    variance = jnp.mean(centred * centred, axis=-1, keepdims=True)
    return centred * lax.rsqrt(variance + EPSILON) * gain + shift


def layer_norm_back(grad, rows, gain):
    mean = jnp.mean(rows, axis=-1, keepdims=True)
    centred = rows - mean
    variance = jnp.mean(centred * centred, axis=-1, keepdims=True)
    inverse = lax.rsqrt(variance + EPSILON)
    hat = centred * inverse
    grad_hat = grad * gain
    grad_rows = inverse * (
        grad_hat
        - jnp.mean(grad_hat, axis=-1, keepdims=True)
        - hat * jnp.mean(grad_hat * hat, axis=-1, keepdims=True)
    )
    return grad_rows, jnp.sum(grad * hat, axis=0), jnp.sum(grad, axis=0)


def make_body(n_fa, n_fb, n_h, n_m):
    n_f, n_z = n_fa * n_fb, n_h * n_m
    n_chip, n_s = n_f * n_z, 2 * n_z
    team = 2 * n_m
    width = WIDE // team
    pairs = width // PAIR
    extra = PAIR

    def team_rows(value):
        pieces = []
        for step in range(n_m):
            part = lax.ppermute(value, "m", shift_perm(n_m, step)) if step else value
            pieces += [part, swap_core(part)]
        return pieces

    def chip_sums(make):
        sums = []
        for step in range(n_m):
            part = make(step)
            half = part.shape[0] // 2
            sums.append(part[:half] + swap_core(part[half:].astype(BF)).astype(F32))
        return sums

    def team_sum(sums):
        total = sums[0]
        for step in range(1, n_m):
            part = lax.ppermute(sums[step].astype(BF), "m", shift_perm(n_m, -step))
            total = total + part.astype(F32)
        return total

    def pair_up(first, second):
        shape = first.shape[:-1]
        first = first.reshape(shape + (pairs, 1, PAIR))
        second = second.reshape(shape + (pairs, 1, PAIR))
        return jnp.concatenate([first, second], axis=-2).reshape(shape + (2 * width,))

    def body(
        layer_input,
        documents,
        cotangent,
        attend_weight,
        attend_bias,
        output_weight,
        output_bias,
        norm_gain,
        norm_shift,
        expand_weight,
        expand_bias,
        reduce_weight,
        reduce_bias,
    ):
        core, half = lax.axis_index("c"), lax.axis_index("h")
        rank = lax.axis_index(("m", "c"))
        layers = attend_weight.shape[0]
        own_rows = 2 * layer_input.shape[1]
        tokens = layer_input.shape[1]
        rows0 = attend_weight.shape[2]
        rows1 = 2 * rows0
        units = reduce_weight.shape[1]
        lots = units // rows0
        lanes_of = 8 + lots

        def by_core(own, other, axis):
            return jnp.where(
                core == 0,
                jnp.concatenate([own, other], axis=axis),
                jnp.concatenate([other, own], axis=axis),
            )

        def to_halves(pair):
            keep = jnp.where(half == 0, pair[0], pair[1])
            give = jnp.where(half == 0, pair[1], pair[0])
            got = lax.ppermute(give, "h", [(0, 1), (1, 0)])
            first = jnp.where(half == 0, keep, got)
            last = jnp.where(half == 0, got, keep)
            return jnp.concatenate([first, last], axis=0)

        def from_halves(rows):
            first, last = rows[:tokens], rows[tokens:]
            keep = jnp.where(half == 0, first, last)
            give = jnp.where(half == 0, last, first)
            got = lax.ppermute(give, "h", [(0, 1), (1, 0)])
            return jnp.where(half == 0, jnp.stack([keep, got]), jnp.stack([got, keep]))

        def small_lanes(layer):
            return jnp.concatenate(
                [
                    attend_bias[layer],
                    output_bias[layer][None],
                    norm_gain[layer],
                    norm_shift[layer],
                    reduce_bias[layer][None],
                    expand_bias[layer].reshape(lots, rows0),
                ],
                axis=0,
            )

        small = jnp.concatenate([small_lanes(layer) for layer in range(layers)], axis=0)
        small = together(small)[0].astype(BF).T
        small = jnp.pad(small, ((0, 0), (0, extra - layers * lanes_of)))

        def attn_shard():
            wa = attend_weight.astype(BF).reshape(layers, 3, rows0, team, width)
            wo = output_weight.astype(BF).reshape(layers, rows0, team, width)
            packed = []
            for layer in range(layers):
                packed += [pair_up(wa[layer, 0], wa[layer, 1]), wa[layer, 2], wo[layer]]
                if layer == 0:
                    packed.append(jnp.broadcast_to(small[:, None], (rows0, team, extra)))
            packed = jnp.swapaxes(jnp.concatenate(packed, axis=-1), 0, 1)
            return jnp.broadcast_to(packed[None], (n_h,) + packed.shape).reshape((n_s,) + packed.shape[1:])

        def column_attn(shard):
            column = lax.all_to_all(shard, ("h", "m", "c"), 0, 0, tiled=True)
            return column.reshape(n_s * rows0, -1)

        def gather_attn(column):
            first, second = column[:, : 2 * width], column[:, 2 * width :]
            first = gather_shift(gather_shift(first, "fb", n_fb, 0), "fa", n_fa, 0)
            second = gather_shift(gather_shift(second, "fa", n_fa, 0), "fb", n_fb, 1)
            first, second = first.reshape(WIDE, -1), second.reshape(WIDE, -1)
            out = second[:, width : 2 * width].reshape(team, width, width)
            out = lax.all_to_all(out, ("m", "c"), 0, 0, tiled=True)
            out = jnp.swapaxes(out, 0, 1).reshape(width, WIDE)
            return (first, second[:, :width], out), second[:, 2 * width :]

        def ffn_shard(layer):
            w1 = expand_weight[layer].astype(BF).reshape(rows0, -1, 2, units)
            own = jnp.where(core == 0, w1[:, :, 0], w1[:, :, 1]).reshape(rows0, 2, WIDE)
            give = jnp.where(core == 0, w1[:, :, 1], w1[:, :, 0]).reshape(rows0, 2, WIDE)
            own, give = jnp.swapaxes(own, 0, 1), jnp.swapaxes(give, 0, 1)
            w1 = by_core(own, swap_core(give), 1).reshape(2 * rows1, WIDE)
            return w1, reduce_weight[layer].astype(BF)

        def column_ffn(shard):
            return gather_shift(shard, ("h", "m"), n_z, 0)

        def gather_ffn(column):
            return lax.all_gather(column, ("fa", "fb"), axis=0, tiled=True)

        attn_w, ffn_w = [None] * layers, [None] * layers
        rows_low = to_halves(layer_input)
        parts = team_rows(rows_low)
        column = column_attn(attn_shard())
        column, parts, (first, second) = together(column, parts, ffn_shard(0))
        first, second = together(column_ffn(first), second)
        second = column_ffn(second)
        attn_w[0], small_all = gather_attn(column[:, : 4 * width + extra])

        small_all = small_all.T.astype(F32)

        def small_params(layer):
            part = small_all[layer * lanes_of : (layer + 1) * lanes_of]
            bias1 = jnp.swapaxes(part[8:].reshape(lots, n_chip, 2, rows0), 0, 1)
            bias1 = jnp.swapaxes(bias1, 1, 2)
            bias1 = jnp.where(core == 0, bias1[:, 0], bias1[:, 1]).reshape(-1)
            return [part[index] for index in range(8)] + [bias1]

        vectors = [small_params(layer) for layer in range(layers)]

        def own_width(vector):
            return lax.dynamic_slice_in_dim(vector, rank * width, width)

        docs = jnp.concatenate(team_rows(to_halves(documents)))
        scale = pair_up(jnp.full((width,), HEAD ** (-0.5), F32), jnp.ones((width,), F32))

        kept = []
        rows_in = rows_low.astype(F32)
        for layer in range(layers):
            qk_w, v_w, out_w = attn_w[layer]
            bq, bv, bo, gain0, gain1, shift0, shift1, bias2, bias1 = vectors[layer]
            bias_qk = pair_up(own_width(bq), jnp.zeros((width,), F32))
            bias_v = own_width(bv)
            if layer:
                parts = team_rows(rows_low)
            qk, value = project_forward(parts, qk_w, v_w, bias_qk, scale, bias_v)
            if layer == 0:
                later = column[:, 4 * width + extra :]
                qk, value, second, ffn_part, later = together(qk, value, second, ffn_shard(1), later)
                attn_w[1], _ = gather_attn(later)
                ffn_w[0] = gather_ffn(first), gather_ffn(second)
                ffn_part = column_ffn(jnp.concatenate(ffn_part, axis=0))
            context, logs = attend_forward(qk, value, docs)
            chip_rows = 2 * own_rows
            sums = chip_sums(
                lambda step: matmul(context[step * chip_rows : (step + 1) * chip_rows], out_w)
            )
            first_sum = rows_in + bo + team_sum(sums)
            first_norm = layer_norm(first_sum, gain0, shift0)
            norm_low = first_norm.astype(BF)
            if layer == 0:
                norm_low, ffn_part = together(norm_low, ffn_part)
                ffn_part = gather_ffn(ffn_part)
                ffn_w[1] = (ffn_part, ffn_part)
            chip_norm = (norm_low, swap_core(norm_low))
            reduced, give, *saved = ffn_forward(chip_norm, ffn_w[layer], bias1)
            second_sum = first_norm + (reduced + swap_core(give).astype(F32) + bias2)
            rows_in = layer_norm(second_sum, gain1, shift1)
            kept.append((parts, qk, value, context, logs, first_sum, saved, second_sum))
            rows_low = rows_in.astype(BF)
            if layer == 0:
                rows_low, cotangent = together(rows_low, cotangent)
                grad_rows = to_halves(cotangent).astype(F32)
        layer_output = from_halves(rows_low)

        def own_first(mine):
            w1 = mine.reshape(layers, 2, rows1, WIDE)
            keep = jnp.where(core == 0, w1[:, :, :rows0], w1[:, :, rows0:])
            give = jnp.where(core == 0, w1[:, :, rows0:], w1[:, :, :rows0])
            got = swap_core(give)
            keep = jnp.swapaxes(keep, 1, 2).reshape(layers, rows0, -1, 1, units)
            got = jnp.swapaxes(got, 1, 2).reshape(layers, rows0, -1, 1, units)
            return by_core(keep, got, 3).reshape(layers, rows0, -1)

        def scatter_attn(first, second):
            first = first.reshape(n_fa, n_fb, n_s * rows0, -1)
            second = second.reshape(n_fa, n_fb, n_s * rows0, -1)
            first = scatter_shift(first, "fa", n_fa, 0).astype(BF)
            second = scatter_shift(second, "fb", n_fb, 1).astype(BF)
            return first, second

        def finish_attn(first, second):
            first = scatter_shift(first, "fb", n_fb, 0)
            second = scatter_shift(second, "fa", n_fa, 0)
            column = jnp.concatenate([first, second], axis=1).astype(BF)
            return column.reshape(n_s, rows0, -1)

        def own_attn(columns):
            pieces = lax.all_to_all(jnp.concatenate(columns, axis=-1), ("h", "m", "c"), 0, 0, tiled=True)
            pieces = jnp.sum(pieces.reshape((n_h, team, rows0, -1)).astype(F32), axis=0)

            def whole(first, count):
                return jnp.swapaxes(pieces[..., first : first + count], 0, 1).reshape(rows0, team * count)

            def matrices(first):
                qk = whole(first, 2 * width).reshape(rows0, team * pairs, 2, PAIR)
                query, key = qk[:, :, 0].reshape(rows0, WIDE), qk[:, :, 1].reshape(rows0, WIDE)
                first = first + 2 * width
                return jnp.stack([query, key, whole(first, width)]), whole(first + width, width)

            both = [matrices(4 * width * index) for index in range(layers)]
            return both, jnp.sum(pieces[..., 4 * width * layers :], axis=0)

        attn_columns, ffn_mine = [None] * layers, [None] * layers
        small_grads = [None] * layers
        for layer in reversed(range(layers)):
            parts, qk, value, context, logs, first_sum, saved, second_sum = kept[layer]
            (qk_w, v_w, out_w), ffn = attn_w[layer], ffn_w[layer]
            gain0, gain1 = vectors[layer][3], vectors[layer][4]
            grad_second, dgain1, dshift1 = layer_norm_back(grad_rows, second_sum, gain1)
            grad_low = grad_second.astype(BF)
            dbias2 = jnp.sum(grad_low, axis=0, dtype=F32)
            chip_low = (grad_low, swap_core(grad_low))
            if layer + 1 < layers:
                chip_low, attn_half = together(chip_low, attn_half)
            reduced, give, dbias1, dw1, dw2 = ffn_backward(chip_low, saved, ffn)
            if layer + 1 < layers:
                attn_columns[layer + 1] = finish_attn(*attn_half)
                ffn_last = jnp.concatenate(ffn_columns, axis=1)
            ffn_columns = [
                lax.psum_scatter(dw, ("fa", "fb"), scatter_dimension=0, tiled=True) for dw in (dw1, dw2)
            ]
            grad_first = grad_second + (reduced + swap_core(give).astype(F32))
            grad_sum, dgain0, dshift0 = layer_norm_back(grad_first, first_sum, gain0)
            grad_low = grad_sum.astype(BF)
            dbo = jnp.sum(grad_low, axis=0, dtype=F32)
            grads = team_rows(grad_low)
            if layer + 1 < layers:
                grads, ffn_last = together(grads, ffn_last)
                ffn_mine[layer + 1] = scatter_shift(ffn_last, ("h", "m"), n_z, 0)
            grad_context, grad_out = output_backward(grads, context, out_w)
            grad_out = jnp.swapaxes(grad_out.reshape(width, team, width), 0, 1)
            grad_out = lax.all_to_all(grad_out, ("m", "c"), 0, 0, tiled=True).reshape(WIDE, width)
            if layer + 1 == layers:
                grad_context, layer_output = together(grad_context, layer_output)
            dqk, dv = attend_backward(grad_context, qk, value, logs, docs)
            grad_qk, grad_v, own, give = project_backward(parts, dqk, dv, qk_w, v_w)
            if layer + 1 < layers:
                grad_qk, own, give, ffn_mine[layer + 1], attn_columns[layer + 1] = together(
                    grad_qk, own, give, ffn_mine[layer + 1], attn_columns[layer + 1]
                )
            sums = [own[step] + swap_core(give[step]).astype(F32) for step in range(n_m)]
            grad_rows = grad_sum + team_sum(sums)
            dbq = jnp.sum(dqk.reshape(-1, pairs, 2, PAIR)[:, :, 0], axis=0, dtype=F32)
            dbv = jnp.sum(dv, axis=0, dtype=F32)

            def spread(vector):
                blank = jnp.zeros((WIDE,), F32)
                return lax.dynamic_update_slice_in_dim(blank, vector.reshape(-1), rank * width, 0)

            dbias1 = dbias1.reshape(n_chip, 1, lots, rows0)
            dbias1 = by_core(dbias1, jnp.zeros_like(dbias1), 1).reshape(2 * n_chip, lots, rows0)
            dbias1 = jnp.swapaxes(dbias1, 0, 1).reshape(lots, WIDE)
            small_grads[layer] = jnp.concatenate(
                [
                    jnp.stack(
                        [spread(dbq), spread(dbv), dbo, dgain0, dgain1, dshift0, dshift1, dbias2]
                    ),
                    dbias1,
                ]
            )
            second = [grad_v, grad_out]
            if layer == 0:
                lanes = jnp.concatenate(small_grads, axis=0).T.astype(BF)
                second.append(jnp.pad(lanes, ((0, 0), (0, extra - layers * lanes_of))))
            attn_half = scatter_attn(grad_qk, jnp.concatenate(second, axis=1))
        input_gradient = from_halves(grad_rows.astype(BF)).astype(F32)
        first = scatter_shift(ffn_columns[0], ("h", "m"), n_z, 0)
        attn_half, first = together(attn_half, first)
        second = scatter_shift(ffn_columns[1], ("h", "m"), n_z, 0)
        column, second, input_gradient = together(finish_attn(*attn_half), second, input_gradient)
        w1_out = own_first(jnp.stack([first, ffn_mine[1][: 2 * rows1]]))
        w2_out = jnp.stack([second, ffn_mine[1][2 * rows1 :]])
        both, more = own_attn([attn_columns[1], column])

        more = more[:, : layers * lanes_of].T.reshape(layers, lanes_of, rows0)
        return (
            layer_output,
            input_gradient,
            jnp.stack([both[1][0], both[0][0]]),
            more[:, :2],
            jnp.stack([both[1][1], both[0][1]]),
            more[:, 2],
            more[:, 3:5],
            more[:, 5:7],
            w1_out,
            more[:, 8:].reshape(layers, units),
            w2_out,
            more[:, 7],
        )

    return body


def solution(mesh):
    n_f, n_s = mesh.shape["fsdp"], mesh.shape["seq"]
    sizes = (2, n_f // 2, 2, n_s // 4, 2)
    grid = Mesh(mesh.devices.reshape(sizes), ("fa", "fb", "h", "m", "c"))
    fsdp, seq = ("fa", "fb"), ("h", "m", "c")
    both = fsdp + seq
    tokens = P(fsdp, seq, None)
    third, second = P(None, None, both), P(None, both)
    weights = (
        P(None, None, both, None),
        third,
        P(None, both, None),
        second,
        third,
        third,
        P(None, both, None),
        second,
        P(None, both, None),
        second,
    )
    return jax.shard_map(
        make_body(*sizes[:4]),
        mesh=grid,
        in_specs=(tokens, P(fsdp, seq), tokens) + weights,
        out_specs=(tokens, tokens) + weights,
        check_vma=False,
    )
```

```python
import jax
import jax.numpy as jnp
from jax import lax
from jax.experimental import pallas as pl
from jax.experimental.pallas import tpu as pltpu
from jax.sharding import Mesh, PartitionSpec as P

HEAD = 64
PAIR = 2 * HEAD
BLOCK = 256
SUB = 256
FFN_TILE = 512
FFN_BACK_TILE = 512
WIDE = 1024
EPSILON = 1e-05
NEG_FILL = -1e30
ROOT_HALF = 0.7071067811865476
ROOT_TWO_PI = 0.3989422804014327
BF = jnp.bfloat16
F32 = jnp.float32
VMEM_BYTES = 56 * 1024 * 1024

def matmul(left, right):
    return jnp.dot(left, right, preferred_element_type=F32)


def matmul_tn(left, right):
    return lax.dot_general(left, right, (((0,), (0,)), ((), ())), preferred_element_type=F32)


def matmul_nt(left, right):
    return lax.dot_general(left, right, (((1,), (1,)), ((), ())), preferred_element_type=F32)


def params(*semantics):
    return pltpu.CompilerParams(dimension_semantics=semantics or None, vmem_limit_bytes=VMEM_BYTES)


def one_head(value, lane, head):
    mine = lane < HEAD if head == 0 else lane >= HEAD
    return jnp.where(mine, value, jnp.zeros_like(value))


def attend_forward_kernel(q_ref, k_ref, v_ref, col_ref, row_ref, c_ref, log_ref):
    lane = lax.broadcasted_iota(jnp.int32, (BLOCK, PAIR), 1)

    def block(index, carry):
        at = pl.ds(pl.multiple_of(index * BLOCK, BLOCK), BLOCK)
        query = q_ref[at, :]
        allowed = col_ref[at, :] == row_ref[...]
        found, logs = [], []
        for head in (0, 1):
            scores = matmul_nt(one_head(query, lane, head), k_ref[...])
            scores = jnp.where(allowed, scores, NEG_FILL)
            top = jnp.max(scores, axis=1, keepdims=True)
            raised = jnp.exp(scores - top)
            total = jnp.sum(raised, axis=1, keepdims=True)
            found.append(matmul(raised.astype(BF), v_ref[...]) * (1.0 / total))
            logs.append(top + jnp.log(total))
        c_ref[at, :] = jnp.where(lane < HEAD, found[0], found[1]).astype(BF)
        log_ref[:, at] = jnp.where(lane < 1, logs[0], logs[1]).T[:8]
        return carry

    lax.fori_loop(0, q_ref.shape[0] // BLOCK, block, 0)


def pair_specs(tokens):
    return [
        pl.BlockSpec((tokens, PAIR), lambda p: (0, 2 * p)),
        pl.BlockSpec((tokens, PAIR), lambda p: (0, 2 * p + 1)),
        pl.BlockSpec((tokens, PAIR), lambda p: (0, p)),
    ]


def docs_specs(tokens):
    return [
        pl.BlockSpec((tokens, 1), lambda p: (0, 0)),
        pl.BlockSpec((1, tokens), lambda p: (0, 0)),
    ]


def attend_forward(query_key, value, docs):
    tokens, width = value.shape
    pairs = width // PAIR
    return pl.pallas_call(
        attend_forward_kernel,
        grid=(pairs,),
        in_specs=pair_specs(tokens) + docs_specs(tokens),
        out_specs=[
            pl.BlockSpec((tokens, PAIR), lambda p: (0, p)),
            pl.BlockSpec((8, tokens), lambda p: (p, 0)),
        ],
        out_shape=[
            jax.ShapeDtypeStruct((tokens, width), BF),
            jax.ShapeDtypeStruct((8 * pairs, tokens), F32),
        ],
        compiler_params=params("arbitrary"),
        cost_estimate=pl.CostEstimate(
            flops=16 * tokens * tokens * width,
            bytes_accessed=10 * tokens * width,
            transcendentals=tokens * tokens * width // HEAD,
        ),
    )(query_key, query_key, value, docs[:, None], docs[None])


def attend_backward_kernel(
    q_ref, k_ref, v_ref, g_ref, col_ref, row_ref, log_ref, dqk_ref, dv_ref, kt_ref, key_ref, value_ref
):
    lane = lax.broadcasted_iota(jnp.int32, (BLOCK, PAIR), 1)
    down = lax.broadcasted_iota(jnp.int32, (PAIR, BLOCK), 0)
    kt_ref[...] = k_ref[...].T
    key_ref[...] = jnp.zeros_like(key_ref)
    value_ref[...] = jnp.zeros_like(value_ref)

    def block(index, carry):
        at = pl.ds(pl.multiple_of(index * BLOCK, BLOCK), BLOCK)
        query, grad = q_ref[at, :], g_ref[at, :]
        allowed = col_ref[...] == row_ref[:, at]
        found = []
        for head in (0, 1):
            query_one, grad_one = one_head(query, lane, head), one_head(grad, lane, head)
            scores = matmul_nt(k_ref[...], query_one)
            soft = jnp.exp(jnp.where(allowed, scores, NEG_FILL) - log_ref[head : head + 1, at])
            grad_soft = matmul_nt(v_ref[...], grad_one)
            delta = jnp.sum(soft * grad_soft, axis=0, keepdims=True)
            low = (soft * (grad_soft - delta)).astype(BF)
            value_ref[...] += matmul(soft.astype(BF), grad_one)
            key_ref[...] += matmul(low, query_one)
            found.append(matmul(kt_ref[...], low))
        dq = jnp.where(down < HEAD, found[0], found[1]) * HEAD ** (-0.5)
        dqk_ref[at, :PAIR] = dq.T.astype(BF)
        return carry

    lax.fori_loop(0, q_ref.shape[0] // BLOCK, block, 0)
    dqk_ref[:, PAIR:] = key_ref[...].astype(BF)
    dv_ref[...] = value_ref[...].astype(BF)


def attend_backward(grad, query_key, value, logs, docs):
    tokens, width = grad.shape
    pairs = width // PAIR
    return pl.pallas_call(
        attend_backward_kernel,
        grid=(pairs,),
        in_specs=pair_specs(tokens)
        + [pl.BlockSpec((tokens, PAIR), lambda p: (0, p))]
        + docs_specs(tokens)
        + [pl.BlockSpec((8, tokens), lambda p: (p, 0))],
        out_specs=[
            pl.BlockSpec((tokens, 2 * PAIR), lambda p: (0, p)),
            pl.BlockSpec((tokens, PAIR), lambda p: (0, p)),
        ],
        out_shape=[
            jax.ShapeDtypeStruct((tokens, 2 * width), BF),
            jax.ShapeDtypeStruct((tokens, width), BF),
        ],
        scratch_shapes=[
            pltpu.VMEM((PAIR, tokens), BF),
            pltpu.VMEM((tokens, PAIR), F32),
            pltpu.VMEM((tokens, PAIR), F32),
        ],
        compiler_params=params("arbitrary"),
        cost_estimate=pl.CostEstimate(
            flops=40 * tokens * tokens * width,
            bytes_accessed=18 * tokens * width,
            transcendentals=tokens * tokens * width // HEAD,
        ),
    )(query_key, query_key, value, grad, docs[:, None], docs[None], logs)


def ffn_forward_kernel(
    x0_ref, x1_ref, w1_ref, w2_ref, b_ref, own_ref, give_ref, gt_ref, slope_ref, xt_ref, x_ref, total_ref
):
    step = pl.program_id(0)
    tile = b_ref.shape[1]

    @pl.when(step == 0)
    def _():
        half = x0_ref.shape[0]
        x_ref[:half, :] = x0_ref[...]
        x_ref[half:, :] = x1_ref[...]
        xt_ref[...] = x_ref[...].T
        total_ref[...] = jnp.zeros_like(total_ref)

    part = 0.0
    for first in range(0, tile, SUB):
        lanes = slice(first, first + SUB)
        group = w2_ref.shape[0] * SUB // tile
        chips = slice(first * w2_ref.shape[0] // tile, first * w2_ref.shape[0] // tile + group)
        expanded = matmul(x_ref[...], w1_ref[:, :, lanes].reshape(WIDE, SUB)) + b_ref[:, lanes]
        normal = 0.5 + 0.5 * lax.erf(expanded * ROOT_HALF)
        slope_ref[:, lanes] = normal + expanded * (ROOT_TWO_PI * jnp.exp(-0.5 * expanded * expanded))
        active = (expanded * normal).astype(BF)
        gt_ref[lanes, :] = active.T
        part = part + matmul(active, w2_ref[chips].reshape(SUB, WIDE))
    total_ref[...] += part

    @pl.when(step == pl.num_programs(0) - 1)
    def _():
        half = own_ref.shape[0]
        own_ref[...] = total_ref[:half, :]
        give_ref[...] = total_ref[half:, :].astype(BF)


def ffn_specs(weights, tile):
    chips = weights[0].shape[0]
    rows = (2 * WIDE) // chips
    per_half = WIDE // tile
    place = weights[1].shape[1] // rows - 1
    return [
        pl.BlockSpec((chips, rows // 2, tile), lambda t: (0, t // per_half, t % per_half)),
        pl.BlockSpec((tile // rows, rows, WIDE), lambda t: (t, place, 0)),
    ]


def ffn_forward(rows_low, weights, bias):
    tokens, tile = 2 * rows_low[0].shape[0], FFN_TILE
    half = pl.BlockSpec((tokens // 2, WIDE), lambda t: (0, 0))
    return pl.pallas_call(
        ffn_forward_kernel,
        grid=(2 * WIDE // tile,),
        in_specs=[half, half]
        + ffn_specs(weights, tile)
        + [pl.BlockSpec((1, tile), lambda t: (0, t))],
        out_specs=[
            half,
            half,
            pl.BlockSpec((tile, tokens), lambda t: (t, 0)),
            pl.BlockSpec((tokens, tile), lambda t: (0, t)),
            pl.BlockSpec((WIDE, tokens), lambda t: (0, 0)),
        ],
        out_shape=[
            jax.ShapeDtypeStruct((tokens // 2, WIDE), F32),
            jax.ShapeDtypeStruct((tokens // 2, WIDE), BF),
            jax.ShapeDtypeStruct((2 * WIDE, tokens), BF),
            jax.ShapeDtypeStruct((tokens, 2 * WIDE), F32),
            jax.ShapeDtypeStruct((WIDE, tokens), BF),
        ],
        scratch_shapes=[pltpu.VMEM((tokens, WIDE), BF), pltpu.VMEM((tokens, WIDE), F32)],
        compiler_params=params("arbitrary"),
        cost_estimate=pl.CostEstimate(
            flops=8 * tokens * WIDE * WIDE,
            bytes_accessed=16 * WIDE * WIDE + 16 * tokens * WIDE,
            transcendentals=4 * tokens * WIDE,
        ),
    )(*rows_low, *weights, bias[None])


def ffn_backward_kernel(
    g0_ref,
    g1_ref,
    xt_ref,
    gt_ref,
    slope_ref,
    w1_ref,
    w2_ref,
    own_ref,
    give_ref,
    db_ref,
    dw1_ref,
    dw2_ref,
    g_ref,
    total_ref,
):
    step = pl.program_id(0)
    tile = slope_ref.shape[1]

    @pl.when(step == 0)
    def _():
        half = g0_ref.shape[0]
        g_ref[:half, :] = g0_ref[...]
        g_ref[half:, :] = g1_ref[...]
        total_ref[...] = jnp.zeros_like(total_ref)

    grad = g_ref[...]
    low = (matmul_nt(grad, w2_ref[...].reshape(tile, WIDE)) * slope_ref[...]).astype(BF)
    dw2_ref[...] = matmul(gt_ref[...], grad).astype(BF).reshape(dw2_ref.shape)
    db_ref[...] = jnp.sum(low.astype(F32), axis=0, keepdims=True)
    dw1_ref[...] = matmul(xt_ref[...], low).astype(BF).reshape(dw1_ref.shape)
    total_ref[...] += matmul_nt(low, w1_ref[...].reshape(WIDE, tile))

    @pl.when(step == pl.num_programs(0) - 1)
    def _():
        half = own_ref.shape[0]
        own_ref[...] = total_ref[:half, :]
        give_ref[...] = total_ref[half:, :].astype(BF)


def ffn_backward(grad_low, saved, weights):
    tokens, tile = 2 * grad_low[0].shape[0], FFN_BACK_TILE
    half = pl.BlockSpec((tokens // 2, WIDE), lambda t: (0, 0))
    active_t, slope, rows_t = saved
    chips = weights[0].shape[0]
    matrix = (chips, 2 * WIDE // chips, WIDE)
    return pl.pallas_call(
        ffn_backward_kernel,
        grid=(2 * WIDE // tile,),
        in_specs=[
            half,
            half,
            pl.BlockSpec((WIDE, tokens), lambda t: (0, 0)),
            pl.BlockSpec((tile, tokens), lambda t: (t, 0)),
            pl.BlockSpec((tokens, tile), lambda t: (0, t)),
        ]
        + ffn_specs(weights, tile),
        out_specs=[
            half,
            half,
            pl.BlockSpec((1, tile), lambda t: (0, t)),
        ]
        + ffn_specs((jax.ShapeDtypeStruct(matrix, BF),) * 2, tile),
        out_shape=[
            jax.ShapeDtypeStruct((tokens // 2, WIDE), F32),
            jax.ShapeDtypeStruct((tokens // 2, WIDE), BF),
            jax.ShapeDtypeStruct((1, 2 * WIDE), F32),
            jax.ShapeDtypeStruct(matrix, BF),
            jax.ShapeDtypeStruct(matrix, BF),
        ],
        scratch_shapes=[pltpu.VMEM((tokens, WIDE), BF), pltpu.VMEM((tokens, WIDE), F32)],
        compiler_params=params("arbitrary"),
        cost_estimate=pl.CostEstimate(
            flops=16 * tokens * WIDE * WIDE,
            bytes_accessed=32 * WIDE * WIDE + 20 * tokens * WIDE,
            transcendentals=0,
        ),
    )(*grad_low, rows_t, active_t, slope, *weights)


def project_forward_kernel(*refs):
    *x_refs, qk_ref, v_ref, bqk_ref, scale_ref, bv_ref, qk_out, v_out = refs
    for index, x_ref in enumerate(x_refs):
        rows = x_ref[...]
        at = slice(index * rows.shape[0], (index + 1) * rows.shape[0])
        qk_out[at, :] = ((matmul(rows, qk_ref[...]) + bqk_ref[...]) * scale_ref[...]).astype(BF)
        v_out[at, :] = (matmul(rows, v_ref[...]) + bv_ref[...]).astype(BF)


def project_forward(pieces, qk_w, v_w, bias_qk, scale, bias_v):
    tokens, width = len(pieces) * pieces[0].shape[0], v_w.shape[1]
    return pl.pallas_call(
        project_forward_kernel,
        out_shape=[
            jax.ShapeDtypeStruct((tokens, 2 * width), BF),
            jax.ShapeDtypeStruct((tokens, width), BF),
        ],
        compiler_params=params(),
        cost_estimate=pl.CostEstimate(
            flops=6 * tokens * WIDE * width,
            bytes_accessed=2 * tokens * (WIDE + 3 * width) + 6 * WIDE * width,
            transcendentals=0,
        ),
    )(*pieces, qk_w, v_w, bias_qk[None], scale[None], bias_v[None])


def project_backward_kernel(*refs):
    *x_refs, dqk_ref, dv_ref, qk_ref, v_ref, gqk_ref, gv_ref, own_ref, give_ref, xt_ref = refs
    rows = x_refs[0].shape[0]
    for index, x_ref in enumerate(x_refs):
        at = slice(index * rows, (index + 1) * rows)
        xt_ref[:, at] = x_ref[...].T
        found = matmul_nt(dqk_ref[at, :], qk_ref[...]) + matmul_nt(dv_ref[at, :], v_ref[...])
        if index % 2 == 0:
            own_ref[index // 2] = found
        else:
            give_ref[index // 2] = found.astype(BF)
    gqk_ref[...] = matmul(xt_ref[...], dqk_ref[...]).astype(BF)
    gv_ref[...] = matmul(xt_ref[...], dv_ref[...]).astype(BF)


def project_backward(pieces, dqk, dv, qk_w, v_w):
    count, rows, width = len(pieces), pieces[0].shape[0], dv.shape[1]
    return pl.pallas_call(
        project_backward_kernel,
        out_shape=[
            jax.ShapeDtypeStruct((WIDE, 2 * width), BF),
            jax.ShapeDtypeStruct((WIDE, width), BF),
            jax.ShapeDtypeStruct((count // 2, rows, WIDE), F32),
            jax.ShapeDtypeStruct((count // 2, rows, WIDE), BF),
        ],
        scratch_shapes=[pltpu.VMEM((WIDE, count * rows), BF)],
        compiler_params=params(),
        cost_estimate=pl.CostEstimate(
            flops=12 * count * rows * WIDE * width,
            bytes_accessed=8 * count * rows * WIDE + 12 * WIDE * width,
            transcendentals=0,
        ),
    )(*pieces, dqk, dv, qk_w, v_w)


def output_backward_kernel(*refs):
    *g_refs, context_ref, out_ref, gcontext_ref, gout_ref = refs
    rows = g_refs[0].shape[0]
    total = 0.0
    for index, g_ref in enumerate(g_refs):
        at = slice(index * rows, (index + 1) * rows)
        gcontext_ref[at, :] = matmul_nt(g_ref[...], out_ref[...]).astype(BF)
        total = total + matmul(context_ref[at, :].T, g_ref[...])
    gout_ref[...] = total.astype(BF)


def output_backward(grads, context, out_w):
    return pl.pallas_call(
        output_backward_kernel,
        out_shape=[
            jax.ShapeDtypeStruct(context.shape, BF),
            jax.ShapeDtypeStruct(out_w.shape, BF),
        ],
        compiler_params=params(),
        cost_estimate=pl.CostEstimate(
            flops=4 * context.shape[0] * context.shape[1] * WIDE,
            bytes_accessed=2 * context.shape[0] * WIDE + 8 * context.shape[1] * WIDE,
            transcendentals=0,
        ),
    )(*grads, context, out_w)


def shift_perm(count, step):
    return [(i, (i + step) % count) for i in range(count)]


def swap_core(value):
    return lax.ppermute(value, "c", [(0, 1), (1, 0)])


def pieces_shift(value, axis, count):
    return [value] + [lax.ppermute(value, axis, shift_perm(count, step)) for step in range(1, count)]


def place_shift(pieces, axis, dim):
    value, count = pieces[0], len(pieces)
    place = lax.axis_index(axis)
    out = jnp.zeros(value.shape[:dim] + (count,) + value.shape[dim:], value.dtype)
    for step, piece in enumerate(pieces):
        out = lax.dynamic_update_index_in_dim(out, piece, (place - step) % count, dim)
    return out


def gather_shift(value, axis, count, dim):
    return place_shift(pieces_shift(value, axis, count), axis, dim)


def scatter_shift(value, axis, count, dim):
    place = lax.axis_index(axis)

    def piece(step):
        return lax.dynamic_index_in_dim(value, (place + step) % count, dim, keepdims=False)

    got = [lax.ppermute(piece(step), axis, shift_perm(count, step)) for step in range(1, count)]
    total = piece(0).astype(F32)
    for part in got:
        total = total + part.astype(F32)
    return total


def together(*values):
    return lax.optimization_barrier(values)


def layer_norm(rows, gain, shift):
    mean = jnp.mean(rows, axis=-1, keepdims=True)
    centred = rows - mean
    variance = jnp.mean(centred * centred, axis=-1, keepdims=True)
    return centred * lax.rsqrt(variance + EPSILON) * gain + shift


def layer_norm_back(grad, rows, gain):
    mean = jnp.mean(rows, axis=-1, keepdims=True)
    centred = rows - mean
    variance = jnp.mean(centred * centred, axis=-1, keepdims=True)
    inverse = lax.rsqrt(variance + EPSILON)
    hat = centred * inverse
    grad_hat = grad * gain
    grad_rows = inverse * (
        grad_hat
        - jnp.mean(grad_hat, axis=-1, keepdims=True)
        - hat * jnp.mean(grad_hat * hat, axis=-1, keepdims=True)
    )
    return grad_rows, jnp.sum(grad * hat, axis=0), jnp.sum(grad, axis=0)


def make_body(n_fa, n_fb, n_h, n_m):
    n_f, n_z = n_fa * n_fb, n_h * n_m
    n_chip, n_s = n_f * n_z, 2 * n_z
    team = 2 * n_m
    width = WIDE // team
    pairs = width // PAIR
    extra = PAIR

    def team_rows(value):
        pieces = []
        for step in range(n_m):
            part = lax.ppermute(value, "m", shift_perm(n_m, step)) if step else value
            pieces += [part, swap_core(part)]
        return pieces

    def chip_sums(make):
        sums = []
        for step in range(n_m):
            part = make(step)
            half = part.shape[0] // 2
            sums.append(part[:half] + swap_core(part[half:].astype(BF)).astype(F32))
        return sums

    def team_sum(sums):
        total = sums[0]
        for step in range(1, n_m):
            part = lax.ppermute(sums[step].astype(BF), "m", shift_perm(n_m, -step))
            total = total + part.astype(F32)
        return total

    def pair_up(first, second):
        shape = first.shape[:-1]
        first = first.reshape(shape + (pairs, 1, PAIR))
        second = second.reshape(shape + (pairs, 1, PAIR))
        return jnp.concatenate([first, second], axis=-2).reshape(shape + (2 * width,))

    def body(
        layer_input,
        documents,
        cotangent,
        attend_weight,
        attend_bias,
        output_weight,
        output_bias,
        norm_gain,
        norm_shift,
        expand_weight,
        expand_bias,
        reduce_weight,
        reduce_bias,
    ):
        core, half = lax.axis_index("c"), lax.axis_index("h")
        rank = lax.axis_index(("m", "c"))
        layers = attend_weight.shape[0]
        own_rows = 2 * layer_input.shape[1]
        tokens = layer_input.shape[1]
        rows0 = attend_weight.shape[2]
        rows1 = 2 * rows0
        units = reduce_weight.shape[1]
        lots = units // rows0
        lanes_of = 8 + lots

        def by_core(own, other, axis):
            return jnp.where(
                core == 0,
                jnp.concatenate([own, other], axis=axis),
                jnp.concatenate([other, own], axis=axis),
            )

        def to_halves(pair):
            keep = jnp.where(half == 0, pair[0], pair[1])
            give = jnp.where(half == 0, pair[1], pair[0])
            got = lax.ppermute(give, "h", [(0, 1), (1, 0)])
            first = jnp.where(half == 0, keep, got)
            last = jnp.where(half == 0, got, keep)
            return jnp.concatenate([first, last], axis=0)

        def give_halves(rows):
            give = jnp.where(half == 0, rows[tokens:], rows[:tokens])
            return lax.ppermute(give, "h", [(0, 1), (1, 0)])

        def from_halves(rows, got):
            keep = jnp.where(half == 0, rows[:tokens], rows[tokens:])
            return jnp.where(half == 0, jnp.stack([keep, got]), jnp.stack([got, keep]))

        def small_lanes(layer):
            return jnp.concatenate(
                [
                    attend_bias[layer],
                    output_bias[layer][None],
                    norm_gain[layer],
                    norm_shift[layer],
                    reduce_bias[layer][None],
                    expand_bias[layer].reshape(lots, rows0),
                ],
                axis=0,
            )

        small = jnp.concatenate([small_lanes(layer) for layer in range(layers)], axis=0)
        small = together(small)[0].astype(BF).T
        small = jnp.pad(small, ((0, 0), (0, extra - layers * lanes_of)))

        def attn_shard():
            wa = attend_weight.astype(BF).reshape(layers, 3, rows0, team, width)
            wo = output_weight.astype(BF).reshape(layers, rows0, team, width)
            packed = []
            for layer in range(layers):
                packed += [pair_up(wa[layer, 0], wa[layer, 1]), wa[layer, 2], wo[layer]]
                if layer == 0:
                    packed.append(jnp.broadcast_to(small[:, None], (rows0, team, extra)))
            packed = jnp.swapaxes(jnp.concatenate(packed, axis=-1), 0, 1)
            return jnp.broadcast_to(packed[None], (n_h,) + packed.shape).reshape((n_s,) + packed.shape[1:])

        def column_attn(shard):
            column = lax.all_to_all(shard, ("h", "m", "c"), 0, 0, tiled=True)
            return column.reshape(n_s * rows0, -1)

        def half_attn(column):
            first, second = column[:, : 2 * width], column[:, 2 * width :]
            return gather_shift(first, "fb", n_fb, 0), gather_shift(second, "fa", n_fa, 0)

        def pieces_attn(first, second):
            return pieces_shift(first, "fa", n_fa), pieces_shift(second, "fb", n_fb)

        def gather_attn(first, second):
            first = place_shift(first, "fa", 0)
            second = place_shift(second, "fb", 1)
            first, second = first.reshape(WIDE, -1), second.reshape(WIDE, -1)
            out = second[:, width : 2 * width].reshape(team, width, width)
            out = lax.all_to_all(out, ("m", "c"), 0, 0, tiled=True)
            out = jnp.swapaxes(out, 0, 1).reshape(width, WIDE)
            return (first, second[:, :width], out), second[:, 2 * width :]

        def ffn_shard(layer):
            w1 = expand_weight[layer].astype(BF).reshape(rows0, -1, 2, units)
            own = jnp.where(core == 0, w1[:, :, 0], w1[:, :, 1]).reshape(rows0, 2, WIDE)
            give = jnp.where(core == 0, w1[:, :, 1], w1[:, :, 0]).reshape(rows0, 2, WIDE)
            own, give = jnp.swapaxes(own, 0, 1), jnp.swapaxes(give, 0, 1)
            w1 = by_core(own, swap_core(give), 1).reshape(2 * rows1, WIDE)
            return w1, reduce_weight[layer].astype(BF)

        def column_ffn(shard):
            return gather_shift(shard, ("h", "m"), n_z, 0)

        def gather_ffn(column):
            return lax.all_gather(column, ("fa", "fb"), axis=0, tiled=True)

        attn_w, ffn_w = [None] * layers, [None] * layers
        rows_low = to_halves(layer_input)
        parts = team_rows(rows_low)
        column = column_attn(attn_shard())
        docs = team_rows(to_halves(documents))
        column, parts, docs, (first, second) = together(column, parts, docs, ffn_shard(0))
        halves = half_attn(column[:, : 4 * width + extra])
        first, second, halves = together(column_ffn(first), second, halves)
        second = column_ffn(second)
        attn_w[0], small_all = gather_attn(*pieces_attn(*halves))

        small_all = small_all.T.astype(F32)

        def small_params(layer):
            part = small_all[layer * lanes_of : (layer + 1) * lanes_of]
            bias1 = jnp.swapaxes(part[8:].reshape(lots, n_chip, 2, rows0), 0, 1)
            bias1 = jnp.swapaxes(bias1, 1, 2)
            bias1 = jnp.where(core == 0, bias1[:, 0], bias1[:, 1]).reshape(-1)
            return [part[index] for index in range(8)] + [bias1]

        vectors = [small_params(layer) for layer in range(layers)]

        def own_width(vector):
            return lax.dynamic_slice_in_dim(vector, rank * width, width)

        docs = jnp.concatenate(docs)
        scale = pair_up(jnp.full((width,), HEAD ** (-0.5), F32), jnp.ones((width,), F32))

        kept = []
        rows_in = rows_low.astype(F32)
        for layer in range(layers):
            qk_w, v_w, out_w = attn_w[layer]
            bq, bv, bo, gain0, gain1, shift0, shift1, bias2, bias1 = vectors[layer]
            bias_qk = pair_up(own_width(bq), jnp.zeros((width,), F32))
            bias_v = own_width(bv)
            if layer:
                parts = team_rows(rows_low)
            qk, value = project_forward(parts, qk_w, v_w, bias_qk, scale, bias_v)
            if layer == 0:
                later = column[:, 4 * width + extra :]
                qk, value, second, ffn_part, later = together(qk, value, second, ffn_shard(1), later)
                attn_w[1], _ = gather_attn(*pieces_attn(*half_attn(later)))
                ffn_w[0] = gather_ffn(first), gather_ffn(second)
                ffn_part = column_ffn(jnp.concatenate(ffn_part, axis=0))
            context, logs = attend_forward(qk, value, docs)
            chip_rows = 2 * own_rows
            sums = chip_sums(
                lambda step: matmul(context[step * chip_rows : (step + 1) * chip_rows], out_w)
            )
            first_sum = rows_in + bo + team_sum(sums)
            first_norm = layer_norm(first_sum, gain0, shift0)
            norm_low = first_norm.astype(BF)
            if layer == 0:
                norm_low, ffn_part = together(norm_low, ffn_part)
                ffn_part = gather_ffn(ffn_part)
                ffn_w[1] = (ffn_part, ffn_part)
            chip_norm = (norm_low, swap_core(norm_low))
            if layer:
                chip_norm, grad_rows = together(chip_norm, grad_rows)
            reduced, give, *saved = ffn_forward(chip_norm, ffn_w[layer], bias1)
            second_sum = first_norm + (reduced + swap_core(give).astype(F32) + bias2)
            rows_in = layer_norm(second_sum, gain1, shift1)
            kept.append((parts, qk, value, context, logs, first_sum, saved, second_sum))
            rows_low = rows_in.astype(BF)
            if layer == 0:
                rows_low, cotangent = together(rows_low, cotangent)
                grad_rows = to_halves(cotangent).astype(F32)
        output_got = give_halves(rows_low)

        def own_first(mine):
            w1 = mine.reshape(layers, 2, rows1, WIDE)
            keep = jnp.where(core == 0, w1[:, :, :rows0], w1[:, :, rows0:])
            give = jnp.where(core == 0, w1[:, :, rows0:], w1[:, :, :rows0])
            got = swap_core(give)
            keep = jnp.swapaxes(keep, 1, 2).reshape(layers, rows0, -1, 1, units)
            got = jnp.swapaxes(got, 1, 2).reshape(layers, rows0, -1, 1, units)
            return by_core(keep, got, 3).reshape(layers, rows0, -1)

        def scatter_attn(first, second):
            first = first.reshape(n_fa, n_fb, n_s * rows0, -1)
            second = second.reshape(n_fa, n_fb, n_s * rows0, -1)
            first = scatter_shift(first, "fa", n_fa, 0).astype(BF)
            second = scatter_shift(second, "fb", n_fb, 1).astype(BF)
            return first, second

        def finish_attn(first, second):
            first = scatter_shift(first, "fb", n_fb, 0)
            second = scatter_shift(second, "fa", n_fa, 0)
            column = jnp.concatenate([first, second], axis=1).astype(BF)
            return column.reshape(n_s, rows0, -1)

        def own_attn(columns):
            pieces = lax.all_to_all(jnp.concatenate(columns, axis=-1), ("h", "m", "c"), 0, 0, tiled=True)
            pieces = jnp.sum(pieces.reshape((n_h, team, rows0, -1)).astype(F32), axis=0)

            def whole(first, count):
                return jnp.swapaxes(pieces[..., first : first + count], 0, 1).reshape(rows0, team * count)

            def matrices(first):
                qk = whole(first, 2 * width).reshape(rows0, team * pairs, 2, PAIR)
                query, key = qk[:, :, 0].reshape(rows0, WIDE), qk[:, :, 1].reshape(rows0, WIDE)
                first = first + 2 * width
                return jnp.stack([query, key, whole(first, width)]), whole(first + width, width)

            both = [matrices(4 * width * index) for index in range(layers)]
            return both, jnp.sum(pieces[..., 4 * width * layers :], axis=0)

        attn_columns = [None] * layers
        small_grads = [None] * layers
        for layer in reversed(range(layers)):
            parts, qk, value, context, logs, first_sum, saved, second_sum = kept[layer]
            (qk_w, v_w, out_w), ffn = attn_w[layer], ffn_w[layer]
            gain0, gain1 = vectors[layer][3], vectors[layer][4]
            grad_second, dgain1, dshift1 = layer_norm_back(grad_rows, second_sum, gain1)
            grad_low = grad_second.astype(BF)
            dbias2 = jnp.sum(grad_low, axis=0, dtype=F32)
            chip_low = (grad_low, swap_core(grad_low))
            if layer + 1 < layers:
                chip_low, attn_half = together(chip_low, attn_half)
            reduced, give, dbias1, dw1, dw2 = ffn_backward(chip_low, saved, ffn)
            if layer + 1 < layers:
                attn_columns[layer + 1] = finish_attn(*attn_half)
                ffn_last = jnp.concatenate(ffn_columns, axis=1)
            ffn_columns = [
                lax.psum_scatter(dw, ("fa", "fb"), scatter_dimension=0, tiled=True) for dw in (dw1, dw2)
            ]
            grad_first = grad_second + (reduced + swap_core(give).astype(F32))
            grad_sum, dgain0, dshift0 = layer_norm_back(grad_first, first_sum, gain0)
            grad_low = grad_sum.astype(BF)
            dbo = jnp.sum(grad_low, axis=0, dtype=F32)
            grads = team_rows(grad_low)
            if layer + 1 < layers:
                grads, ffn_last = together(grads, ffn_last)
                ffn_mine = scatter_shift(ffn_last, ("h", "m"), n_z, 0)
            grad_context, grad_out = output_backward(grads, context, out_w)
            grad_out = jnp.swapaxes(grad_out.reshape(width, team, width), 0, 1)
            grad_out = lax.all_to_all(grad_out, ("m", "c"), 0, 0, tiled=True).reshape(WIDE, width)
            dqk, dv = attend_backward(grad_context, qk, value, logs, docs)
            grad_qk, grad_v, own, give = project_backward(parts, dqk, dv, qk_w, v_w)
            if layer + 1 < layers:
                grad_qk, own, give, ffn_mine, attn_columns[layer + 1] = together(
                    grad_qk, own, give, ffn_mine, attn_columns[layer + 1]
                )
            else:
                own, give, output_got = together(own, give, output_got)
            sums = [own[step] + swap_core(give[step]).astype(F32) for step in range(n_m)]
            grad_rows = grad_sum + team_sum(sums)
            dbq = jnp.sum(dqk.reshape(-1, pairs, 2, PAIR)[:, :, 0], axis=0, dtype=F32)
            dbv = jnp.sum(dv, axis=0, dtype=F32)

            def spread(vector):
                blank = jnp.zeros((WIDE,), F32)
                return lax.dynamic_update_slice_in_dim(blank, vector.reshape(-1), rank * width, 0)

            dbias1 = dbias1.reshape(n_chip, 1, lots, rows0)
            dbias1 = by_core(dbias1, jnp.zeros_like(dbias1), 1).reshape(2 * n_chip, lots, rows0)
            dbias1 = jnp.swapaxes(dbias1, 0, 1).reshape(lots, WIDE)
            small_grads[layer] = jnp.concatenate(
                [
                    jnp.stack(
                        [spread(dbq), spread(dbv), dbo, dgain0, dgain1, dshift0, dshift1, dbias2]
                    ),
                    dbias1,
                ]
            )
            second = [grad_v, grad_out]
            if layer == 0:
                lanes = jnp.concatenate(small_grads, axis=0).T.astype(BF)
                second.append(jnp.pad(lanes, ((0, 0), (0, extra - layers * lanes_of))))
            attn_half = scatter_attn(grad_qk, jnp.concatenate(second, axis=1))
        grad_low = grad_rows.astype(BF)
        input_got = give_halves(grad_low)
        first = scatter_shift(ffn_columns[0], ("h", "m"), n_z, 0)
        attn_half, first = together(attn_half, first)
        second = scatter_shift(ffn_columns[1], ("h", "m"), n_z, 0)
        column, second, input_got = together(finish_attn(*attn_half), second, input_got)
        input_gradient = from_halves(grad_low, input_got).astype(F32)
        layer_output = from_halves(rows_low, output_got)
        w1_out = own_first(jnp.stack([first, ffn_mine[: 2 * rows1]]))
        w2_out = jnp.stack([second, ffn_mine[2 * rows1 :]])
        both, more = own_attn([attn_columns[1], column])

        more = more[:, : layers * lanes_of].T.reshape(layers, lanes_of, rows0)
        return (
            layer_output,
            input_gradient,
            jnp.stack([both[1][0], both[0][0]]),
            more[:, :2],
            jnp.stack([both[1][1], both[0][1]]),
            more[:, 2],
            more[:, 3:5],
            more[:, 5:7],
            w1_out,
            more[:, 8:].reshape(layers, units),
            w2_out,
            more[:, 7],
        )

    return body


def solution(mesh):
    n_f, n_s = mesh.shape["fsdp"], mesh.shape["seq"]
    sizes = (2, n_f // 2, 2, n_s // 4, 2)
    grid = Mesh(mesh.devices.reshape(sizes), ("fa", "fb", "h", "m", "c"))
    fsdp, seq = ("fa", "fb"), ("h", "m", "c")
    both = fsdp + seq
    tokens = P(fsdp, seq, None)
    third, second = P(None, None, both), P(None, both)
    weights = (
        P(None, None, both, None),
        third,
        P(None, both, None),
        second,
        third,
        third,
        P(None, both, None),
        second,
        P(None, both, None),
        second,
    )
    return jax.shard_map(
        make_body(*sizes[:4]),
        mesh=grid,
        in_specs=(tokens, P(fsdp, seq), tokens) + weights,
        out_specs=(tokens, tokens) + weights,
        check_vma=False,
    )
```

```python
import jax
import jax.numpy as jnp
from jax import lax
from jax.experimental import pallas as pl
from jax.experimental.pallas import tpu as pltpu
from jax.sharding import Mesh, PartitionSpec as P

HEAD = 64
PAIR = 2 * HEAD
BLOCK = 256
SUB = 256
FFN_TILE = 512
FFN_BACK_TILE = 512
WIDE = 1024
EPSILON = 1e-05
NEG_FILL = -1e30
ROOT_HALF = 0.7071067811865476
ROOT_TWO_PI = 0.3989422804014327
BF = jnp.bfloat16
F32 = jnp.float32
VMEM_BYTES = 56 * 1024 * 1024

def matmul(left, right):
    return jnp.dot(left, right, preferred_element_type=F32)


def matmul_tn(left, right):
    return lax.dot_general(left, right, (((0,), (0,)), ((), ())), preferred_element_type=F32)


def matmul_nt(left, right):
    return lax.dot_general(left, right, (((1,), (1,)), ((), ())), preferred_element_type=F32)


def params(*semantics):
    return pltpu.CompilerParams(dimension_semantics=semantics or None, vmem_limit_bytes=VMEM_BYTES)


def one_head(value, lane, head):
    mine = lane < HEAD if head == 0 else lane >= HEAD
    return jnp.where(mine, value, jnp.zeros_like(value))


def attend_forward_kernel(q_ref, k_ref, v_ref, col_ref, row_ref, c_ref, log_ref):
    lane = lax.broadcasted_iota(jnp.int32, (BLOCK, PAIR), 1)

    def block(index, carry):
        at = pl.ds(pl.multiple_of(index * BLOCK, BLOCK), BLOCK)
        query = q_ref[at, :]
        allowed = col_ref[at, :] == row_ref[...]
        found, logs = [], []
        for head in (0, 1):
            scores = matmul_nt(one_head(query, lane, head), k_ref[...])
            scores = jnp.where(allowed, scores, NEG_FILL)
            top = jnp.max(scores, axis=1, keepdims=True)
            raised = jnp.exp(scores - top)
            total = jnp.sum(raised, axis=1, keepdims=True)
            found.append(matmul(raised.astype(BF), v_ref[...]) * (1.0 / total))
            logs.append(top + jnp.log(total))
        c_ref[at, :] = jnp.where(lane < HEAD, found[0], found[1]).astype(BF)
        log_ref[:, at] = jnp.where(lane < 1, logs[0], logs[1]).T[:8]
        return carry

    lax.fori_loop(0, q_ref.shape[0] // BLOCK, block, 0)


def pair_specs(tokens):
    return [
        pl.BlockSpec((tokens, PAIR), lambda p: (0, 2 * p)),
        pl.BlockSpec((tokens, PAIR), lambda p: (0, 2 * p + 1)),
        pl.BlockSpec((tokens, PAIR), lambda p: (0, p)),
    ]


def docs_specs(tokens):
    return [
        pl.BlockSpec((tokens, 1), lambda p: (0, 0)),
        pl.BlockSpec((1, tokens), lambda p: (0, 0)),
    ]


def attend_forward(query_key, value, docs):
    tokens, width = value.shape
    pairs = width // PAIR
    return pl.pallas_call(
        attend_forward_kernel,
        grid=(pairs,),
        in_specs=pair_specs(tokens) + docs_specs(tokens),
        out_specs=[
            pl.BlockSpec((tokens, PAIR), lambda p: (0, p)),
            pl.BlockSpec((8, tokens), lambda p: (p, 0)),
        ],
        out_shape=[
            jax.ShapeDtypeStruct((tokens, width), BF),
            jax.ShapeDtypeStruct((8 * pairs, tokens), F32),
        ],
        compiler_params=params("arbitrary"),
        cost_estimate=pl.CostEstimate(
            flops=16 * tokens * tokens * width,
            bytes_accessed=10 * tokens * width,
            transcendentals=tokens * tokens * width // HEAD,
        ),
    )(query_key, query_key, value, docs[:, None], docs[None])


def attend_backward_kernel(
    q_ref, k_ref, v_ref, g_ref, col_ref, row_ref, log_ref, dqk_ref, dv_ref, kt_ref, key_ref, value_ref
):
    lane = lax.broadcasted_iota(jnp.int32, (BLOCK, PAIR), 1)
    down = lax.broadcasted_iota(jnp.int32, (PAIR, BLOCK), 0)
    kt_ref[...] = k_ref[...].T
    key_ref[...] = jnp.zeros_like(key_ref)
    value_ref[...] = jnp.zeros_like(value_ref)

    def block(index, carry):
        at = pl.ds(pl.multiple_of(index * BLOCK, BLOCK), BLOCK)
        query, grad = q_ref[at, :], g_ref[at, :]
        allowed = col_ref[...] == row_ref[:, at]
        found = []
        for head in (0, 1):
            query_one, grad_one = one_head(query, lane, head), one_head(grad, lane, head)
            scores = matmul_nt(k_ref[...], query_one)
            soft = jnp.exp(jnp.where(allowed, scores, NEG_FILL) - log_ref[head : head + 1, at])
            grad_soft = matmul_nt(v_ref[...], grad_one)
            delta = jnp.sum(soft * grad_soft, axis=0, keepdims=True)
            low = (soft * (grad_soft - delta)).astype(BF)
            value_ref[...] += matmul(soft.astype(BF), grad_one)
            key_ref[...] += matmul(low, query_one)
            found.append(matmul(kt_ref[...], low))
        dq = jnp.where(down < HEAD, found[0], found[1]) * HEAD ** (-0.5)
        dqk_ref[at, :PAIR] = dq.T.astype(BF)
        return carry

    lax.fori_loop(0, q_ref.shape[0] // BLOCK, block, 0)
    dqk_ref[:, PAIR:] = key_ref[...].astype(BF)
    dv_ref[...] = value_ref[...].astype(BF)


def attend_backward(grad, query_key, value, logs, docs):
    tokens, width = grad.shape
    pairs = width // PAIR
    return pl.pallas_call(
        attend_backward_kernel,
        grid=(pairs,),
        in_specs=pair_specs(tokens)
        + [pl.BlockSpec((tokens, PAIR), lambda p: (0, p))]
        + docs_specs(tokens)
        + [pl.BlockSpec((8, tokens), lambda p: (p, 0))],
        out_specs=[
            pl.BlockSpec((tokens, 2 * PAIR), lambda p: (0, p)),
            pl.BlockSpec((tokens, PAIR), lambda p: (0, p)),
        ],
        out_shape=[
            jax.ShapeDtypeStruct((tokens, 2 * width), BF),
            jax.ShapeDtypeStruct((tokens, width), BF),
        ],
        scratch_shapes=[
            pltpu.VMEM((PAIR, tokens), BF),
            pltpu.VMEM((tokens, PAIR), F32),
            pltpu.VMEM((tokens, PAIR), F32),
        ],
        compiler_params=params("arbitrary"),
        cost_estimate=pl.CostEstimate(
            flops=40 * tokens * tokens * width,
            bytes_accessed=18 * tokens * width,
            transcendentals=tokens * tokens * width // HEAD,
        ),
    )(query_key, query_key, value, grad, docs[:, None], docs[None], logs)


def ffn_forward_kernel(
    x0_ref, x1_ref, w1_ref, w2_ref, b_ref, own_ref, give_ref, gt_ref, slope_ref, xt_ref, x_ref, total_ref
):
    step = pl.program_id(0)
    tile = b_ref.shape[1]

    @pl.when(step == 0)
    def _():
        half = x0_ref.shape[0]
        x_ref[:half, :] = x0_ref[...]
        x_ref[half:, :] = x1_ref[...]
        xt_ref[...] = x_ref[...].T
        total_ref[...] = jnp.zeros_like(total_ref)

    part = 0.0
    for first in range(0, tile, SUB):
        lanes = slice(first, first + SUB)
        group = w2_ref.shape[0] * SUB // tile
        chips = slice(first * w2_ref.shape[0] // tile, first * w2_ref.shape[0] // tile + group)
        expanded = matmul(x_ref[...], w1_ref[:, :, lanes].reshape(WIDE, SUB)) + b_ref[:, lanes]
        normal = 0.5 + 0.5 * lax.erf(expanded * ROOT_HALF)
        slope_ref[:, lanes] = normal + expanded * (ROOT_TWO_PI * jnp.exp(-0.5 * expanded * expanded))
        active = (expanded * normal).astype(BF)
        gt_ref[lanes, :] = active.T
        part = part + matmul(active, w2_ref[chips].reshape(SUB, WIDE))
    total_ref[...] += part

    @pl.when(step == pl.num_programs(0) - 1)
    def _():
        half = own_ref.shape[0]
        own_ref[...] = total_ref[:half, :]
        give_ref[...] = total_ref[half:, :].astype(BF)


def ffn_specs(weights, tile):
    chips = weights[0].shape[0]
    rows = (2 * WIDE) // chips
    per_half = WIDE // tile
    place = weights[1].shape[1] // rows - 1
    return [
        pl.BlockSpec((chips, rows // 2, tile), lambda t: (0, t // per_half, t % per_half)),
        pl.BlockSpec((tile // rows, rows, WIDE), lambda t: (t, place, 0)),
    ]


def ffn_forward(rows_low, weights, bias):
    tokens, tile = 2 * rows_low[0].shape[0], FFN_TILE
    half = pl.BlockSpec((tokens // 2, WIDE), lambda t: (0, 0))
    return pl.pallas_call(
        ffn_forward_kernel,
        grid=(2 * WIDE // tile,),
        in_specs=[half, half]
        + ffn_specs(weights, tile)
        + [pl.BlockSpec((1, tile), lambda t: (0, t))],
        out_specs=[
            half,
            half,
            pl.BlockSpec((tile, tokens), lambda t: (t, 0)),
            pl.BlockSpec((tokens, tile), lambda t: (0, t)),
            pl.BlockSpec((WIDE, tokens), lambda t: (0, 0)),
        ],
        out_shape=[
            jax.ShapeDtypeStruct((tokens // 2, WIDE), F32),
            jax.ShapeDtypeStruct((tokens // 2, WIDE), BF),
            jax.ShapeDtypeStruct((2 * WIDE, tokens), BF),
            jax.ShapeDtypeStruct((tokens, 2 * WIDE), F32),
            jax.ShapeDtypeStruct((WIDE, tokens), BF),
        ],
        scratch_shapes=[pltpu.VMEM((tokens, WIDE), BF), pltpu.VMEM((tokens, WIDE), F32)],
        compiler_params=params("arbitrary"),
        cost_estimate=pl.CostEstimate(
            flops=8 * tokens * WIDE * WIDE,
            bytes_accessed=16 * WIDE * WIDE + 16 * tokens * WIDE,
            transcendentals=4 * tokens * WIDE,
        ),
    )(*rows_low, *weights, bias[None])


def ffn_backward_kernel(
    g0_ref,
    g1_ref,
    xt_ref,
    gt_ref,
    slope_ref,
    w1_ref,
    w2_ref,
    own_ref,
    give_ref,
    db_ref,
    dw1_ref,
    dw2_ref,
    g_ref,
    total_ref,
):
    step = pl.program_id(0)
    tile = slope_ref.shape[1]

    @pl.when(step == 0)
    def _():
        half = g0_ref.shape[0]
        g_ref[:half, :] = g0_ref[...]
        g_ref[half:, :] = g1_ref[...]
        total_ref[...] = jnp.zeros_like(total_ref)

    grad = g_ref[...]
    low = (matmul_nt(grad, w2_ref[...].reshape(tile, WIDE)) * slope_ref[...]).astype(BF)
    dw2_ref[...] = matmul(gt_ref[...], grad).astype(BF).reshape(dw2_ref.shape)
    db_ref[...] = jnp.sum(low.astype(F32), axis=0, keepdims=True)
    dw1_ref[...] = matmul(xt_ref[...], low).astype(BF).reshape(dw1_ref.shape)
    total_ref[...] += matmul_nt(low, w1_ref[...].reshape(WIDE, tile))

    @pl.when(step == pl.num_programs(0) - 1)
    def _():
        half = own_ref.shape[0]
        own_ref[...] = total_ref[:half, :]
        give_ref[...] = total_ref[half:, :].astype(BF)


def ffn_backward(grad_low, saved, weights):
    tokens, tile = 2 * grad_low[0].shape[0], FFN_BACK_TILE
    half = pl.BlockSpec((tokens // 2, WIDE), lambda t: (0, 0))
    active_t, slope, rows_t = saved
    chips = weights[0].shape[0]
    matrix = (chips, 2 * WIDE // chips, WIDE)
    return pl.pallas_call(
        ffn_backward_kernel,
        grid=(2 * WIDE // tile,),
        in_specs=[
            half,
            half,
            pl.BlockSpec((WIDE, tokens), lambda t: (0, 0)),
            pl.BlockSpec((tile, tokens), lambda t: (t, 0)),
            pl.BlockSpec((tokens, tile), lambda t: (0, t)),
        ]
        + ffn_specs(weights, tile),
        out_specs=[
            half,
            half,
            pl.BlockSpec((1, tile), lambda t: (0, t)),
        ]
        + ffn_specs((jax.ShapeDtypeStruct(matrix, BF),) * 2, tile),
        out_shape=[
            jax.ShapeDtypeStruct((tokens // 2, WIDE), F32),
            jax.ShapeDtypeStruct((tokens // 2, WIDE), BF),
            jax.ShapeDtypeStruct((1, 2 * WIDE), F32),
            jax.ShapeDtypeStruct(matrix, BF),
            jax.ShapeDtypeStruct(matrix, BF),
        ],
        scratch_shapes=[pltpu.VMEM((tokens, WIDE), BF), pltpu.VMEM((tokens, WIDE), F32)],
        compiler_params=params("arbitrary"),
        cost_estimate=pl.CostEstimate(
            flops=16 * tokens * WIDE * WIDE,
            bytes_accessed=32 * WIDE * WIDE + 20 * tokens * WIDE,
            transcendentals=0,
        ),
    )(*grad_low, rows_t, active_t, slope, *weights)


def project_forward_kernel(*refs):
    *x_refs, qk_ref, v_ref, bqk_ref, scale_ref, bv_ref, qk_out, v_out = refs
    for index, x_ref in enumerate(x_refs):
        rows = x_ref[...]
        at = slice(index * rows.shape[0], (index + 1) * rows.shape[0])
        qk_out[at, :] = ((matmul(rows, qk_ref[...]) + bqk_ref[...]) * scale_ref[...]).astype(BF)
        v_out[at, :] = (matmul(rows, v_ref[...]) + bv_ref[...]).astype(BF)


def project_forward(pieces, qk_w, v_w, bias_qk, scale, bias_v):
    tokens, width = len(pieces) * pieces[0].shape[0], v_w.shape[1]
    return pl.pallas_call(
        project_forward_kernel,
        out_shape=[
            jax.ShapeDtypeStruct((tokens, 2 * width), BF),
            jax.ShapeDtypeStruct((tokens, width), BF),
        ],
        compiler_params=params(),
        cost_estimate=pl.CostEstimate(
            flops=6 * tokens * WIDE * width,
            bytes_accessed=2 * tokens * (WIDE + 3 * width) + 6 * WIDE * width,
            transcendentals=0,
        ),
    )(*pieces, qk_w, v_w, bias_qk[None], scale[None], bias_v[None])


def project_backward_kernel(*refs):
    *x_refs, dqk_ref, dv_ref, qk_ref, v_ref, gqk_ref, gv_ref, own_ref, give_ref, xt_ref = refs
    rows = x_refs[0].shape[0]
    for index, x_ref in enumerate(x_refs):
        at = slice(index * rows, (index + 1) * rows)
        xt_ref[:, at] = x_ref[...].T
        found = matmul_nt(dqk_ref[at, :], qk_ref[...]) + matmul_nt(dv_ref[at, :], v_ref[...])
        if index % 2 == 0:
            own_ref[index // 2] = found
        else:
            give_ref[index // 2] = found.astype(BF)
    gqk_ref[...] = matmul(xt_ref[...], dqk_ref[...]).astype(BF)
    gv_ref[...] = matmul(xt_ref[...], dv_ref[...]).astype(BF)


def project_backward(pieces, dqk, dv, qk_w, v_w):
    count, rows, width = len(pieces), pieces[0].shape[0], dv.shape[1]
    return pl.pallas_call(
        project_backward_kernel,
        out_shape=[
            jax.ShapeDtypeStruct((WIDE, 2 * width), BF),
            jax.ShapeDtypeStruct((WIDE, width), BF),
            jax.ShapeDtypeStruct((count // 2, rows, WIDE), F32),
            jax.ShapeDtypeStruct((count // 2, rows, WIDE), BF),
        ],
        scratch_shapes=[pltpu.VMEM((WIDE, count * rows), BF)],
        compiler_params=params(),
        cost_estimate=pl.CostEstimate(
            flops=12 * count * rows * WIDE * width,
            bytes_accessed=8 * count * rows * WIDE + 12 * WIDE * width,
            transcendentals=0,
        ),
    )(*pieces, dqk, dv, qk_w, v_w)


def output_backward_kernel(*refs):
    *g_refs, context_ref, out_ref, gcontext_ref, gout_ref = refs
    rows = g_refs[0].shape[0]
    total = 0.0
    for index, g_ref in enumerate(g_refs):
        at = slice(index * rows, (index + 1) * rows)
        gcontext_ref[at, :] = matmul_nt(g_ref[...], out_ref[...]).astype(BF)
        total = total + matmul(context_ref[at, :].T, g_ref[...])
    gout_ref[...] = total.astype(BF)


def output_backward(grads, context, out_w):
    return pl.pallas_call(
        output_backward_kernel,
        out_shape=[
            jax.ShapeDtypeStruct(context.shape, BF),
            jax.ShapeDtypeStruct(out_w.shape, BF),
        ],
        compiler_params=params(),
        cost_estimate=pl.CostEstimate(
            flops=4 * context.shape[0] * context.shape[1] * WIDE,
            bytes_accessed=2 * context.shape[0] * WIDE + 8 * context.shape[1] * WIDE,
            transcendentals=0,
        ),
    )(*grads, context, out_w)


def shift_perm(count, step):
    return [(i, (i + step) % count) for i in range(count)]


def swap_core(value):
    return lax.ppermute(value, "c", [(0, 1), (1, 0)])


def pieces_shift(value, axis, count):
    return [value] + [lax.ppermute(value, axis, shift_perm(count, step)) for step in range(1, count)]


def place_shift(pieces, axis, dim):
    value, count = pieces[0], len(pieces)
    place = lax.axis_index(axis)
    out = jnp.zeros(value.shape[:dim] + (count,) + value.shape[dim:], value.dtype)
    for step, piece in enumerate(pieces):
        out = lax.dynamic_update_index_in_dim(out, piece, (place - step) % count, dim)
    return out


def gather_shift(value, axis, count, dim):
    return place_shift(pieces_shift(value, axis, count), axis, dim)


def scatter_shift(value, axis, count, dim):
    place = lax.axis_index(axis)

    def piece(step):
        return lax.dynamic_index_in_dim(value, (place + step) % count, dim, keepdims=False)

    got = [lax.ppermute(piece(step), axis, shift_perm(count, step)) for step in range(1, count)]
    total = piece(0).astype(F32)
    for part in got:
        total = total + part.astype(F32)
    return total


def together(*values):
    return lax.optimization_barrier(values)


def layer_norm(rows, gain, shift):
    mean = jnp.mean(rows, axis=-1, keepdims=True)
    centred = rows - mean
    variance = jnp.mean(centred * centred, axis=-1, keepdims=True)
    return centred * lax.rsqrt(variance + EPSILON) * gain + shift


def layer_norm_back(grad, rows, gain):
    mean = jnp.mean(rows, axis=-1, keepdims=True)
    centred = rows - mean
    variance = jnp.mean(centred * centred, axis=-1, keepdims=True)
    inverse = lax.rsqrt(variance + EPSILON)
    hat = centred * inverse
    grad_hat = grad * gain
    grad_rows = inverse * (
        grad_hat
        - jnp.mean(grad_hat, axis=-1, keepdims=True)
        - hat * jnp.mean(grad_hat * hat, axis=-1, keepdims=True)
    )
    return grad_rows, jnp.sum(grad * hat, axis=0), jnp.sum(grad, axis=0)


def make_body(n_fa, n_fb, n_h, n_m):
    n_f, n_z = n_fa * n_fb, n_h * n_m
    n_chip, n_s = n_f * n_z, 2 * n_z
    team = 2 * n_m
    width = WIDE // team
    pairs = width // PAIR
    extra = PAIR

    def team_rows(value):
        pieces = []
        for step in range(n_m):
            part = lax.ppermute(value, "m", shift_perm(n_m, step)) if step else value
            pieces += [part, swap_core(part)]
        return pieces

    def chip_sums(make):
        sums = []
        for step in range(n_m):
            part = make(step)
            half = part.shape[0] // 2
            sums.append(part[:half] + swap_core(part[half:].astype(BF)).astype(F32))
        return sums

    def team_sum(sums):
        total = sums[0]
        for step in range(1, n_m):
            part = lax.ppermute(sums[step].astype(BF), "m", shift_perm(n_m, -step))
            total = total + part.astype(F32)
        return total

    def pair_up(first, second):
        shape = first.shape[:-1]
        first = first.reshape(shape + (pairs, 1, PAIR))
        second = second.reshape(shape + (pairs, 1, PAIR))
        return jnp.concatenate([first, second], axis=-2).reshape(shape + (2 * width,))

    def body(
        layer_input,
        documents,
        cotangent,
        attend_weight,
        attend_bias,
        output_weight,
        output_bias,
        norm_gain,
        norm_shift,
        expand_weight,
        expand_bias,
        reduce_weight,
        reduce_bias,
    ):
        core, half = lax.axis_index("c"), lax.axis_index("h")
        rank = lax.axis_index(("m", "c"))
        layers = attend_weight.shape[0]
        own_rows = 2 * layer_input.shape[1]
        tokens = layer_input.shape[1]
        rows0 = attend_weight.shape[2]
        rows1 = 2 * rows0
        units = reduce_weight.shape[1]
        lots = units // rows0
        lanes_of = 8 + lots

        def by_core(own, other, axis):
            return jnp.where(
                core == 0,
                jnp.concatenate([own, other], axis=axis),
                jnp.concatenate([other, own], axis=axis),
            )

        def to_halves(pair):
            keep = jnp.where(half == 0, pair[0], pair[1])
            give = jnp.where(half == 0, pair[1], pair[0])
            got = lax.ppermute(give, "h", [(0, 1), (1, 0)])
            first = jnp.where(half == 0, keep, got)
            last = jnp.where(half == 0, got, keep)
            return jnp.concatenate([first, last], axis=0)

        def give_halves(rows):
            give = jnp.where(half == 0, rows[tokens:], rows[:tokens])
            return lax.ppermute(give, "h", [(0, 1), (1, 0)])

        def from_halves(rows, got):
            keep = jnp.where(half == 0, rows[:tokens], rows[tokens:])
            return jnp.where(half == 0, jnp.stack([keep, got]), jnp.stack([got, keep]))

        def small_lanes(layer):
            return jnp.concatenate(
                [
                    attend_bias[layer],
                    output_bias[layer][None],
                    norm_gain[layer],
                    norm_shift[layer],
                    reduce_bias[layer][None],
                    expand_bias[layer].reshape(lots, rows0),
                ],
                axis=0,
            )

        small = jnp.concatenate([small_lanes(layer) for layer in range(layers)], axis=0)
        small = together(small)[0].astype(BF).T
        small = jnp.pad(small, ((0, 0), (0, extra - layers * lanes_of)))

        def attn_shard():
            wa = attend_weight.astype(BF).reshape(layers, 3, rows0, team, width)
            wo = output_weight.astype(BF).reshape(layers, rows0, team, width)
            packed = []
            for layer in range(layers):
                packed += [pair_up(wa[layer, 0], wa[layer, 1]), wa[layer, 2], wo[layer]]
                if layer == 0:
                    packed.append(jnp.broadcast_to(small[:, None], (rows0, team, extra)))
            packed = jnp.swapaxes(jnp.concatenate(packed, axis=-1), 0, 1)
            return jnp.broadcast_to(packed[None], (n_h,) + packed.shape).reshape((n_s,) + packed.shape[1:])

        def column_attn(shard):
            column = lax.all_to_all(shard, ("h", "m", "c"), 0, 0, tiled=True)
            return column.reshape(n_s * rows0, -1)

        def half_attn(column):
            first, second = column[:, : 2 * width], column[:, 2 * width :]
            return gather_shift(first, "fb", n_fb, 0), gather_shift(second, "fa", n_fa, 0)

        def pieces_attn(first, second):
            return pieces_shift(first, "fa", n_fa), pieces_shift(second, "fb", n_fb)

        def gather_attn(first, second):
            first = place_shift(first, "fa", 0)
            second = place_shift(second, "fb", 1)
            first, second = first.reshape(WIDE, -1), second.reshape(WIDE, -1)
            out = second[:, width : 2 * width].reshape(team, width, width)
            out = lax.all_to_all(out, ("m", "c"), 0, 0, tiled=True)
            out = jnp.swapaxes(out, 0, 1).reshape(width, WIDE)
            return (first, second[:, :width], out), second[:, 2 * width :]

        def ffn_shard(layer):
            w1 = expand_weight[layer].astype(BF).reshape(rows0, -1, 2, units)
            own = jnp.where(core == 0, w1[:, :, 0], w1[:, :, 1]).reshape(rows0, 2, WIDE)
            give = jnp.where(core == 0, w1[:, :, 1], w1[:, :, 0]).reshape(rows0, 2, WIDE)
            own, give = jnp.swapaxes(own, 0, 1), jnp.swapaxes(give, 0, 1)
            w1 = by_core(own, swap_core(give), 1).reshape(2 * rows1, WIDE)
            return w1, reduce_weight[layer].astype(BF)

        def column_ffn(shard):
            return gather_shift(shard, ("h", "m"), n_z, 0)

        def gather_ffn(column):
            return lax.all_gather(column, ("fa", "fb"), axis=0, tiled=True)

        attn_w, ffn_w = [None] * layers, [None] * layers
        rows_low = to_halves(layer_input)
        parts = team_rows(rows_low)
        column = column_attn(attn_shard())
        docs = team_rows(to_halves(documents))
        column, parts, docs, (first, second) = together(column, parts, docs, ffn_shard(0))
        halves = half_attn(column[:, : 4 * width + extra])
        first, second, halves = together(column_ffn(first), second, halves)
        second = column_ffn(second)
        attn_w[0], small_all = gather_attn(*pieces_attn(*halves))

        small_all = small_all.T.astype(F32)

        def small_params(layer):
            part = small_all[layer * lanes_of : (layer + 1) * lanes_of]
            bias1 = jnp.swapaxes(part[8:].reshape(lots, n_chip, 2, rows0), 0, 1)
            bias1 = jnp.swapaxes(bias1, 1, 2)
            bias1 = jnp.where(core == 0, bias1[:, 0], bias1[:, 1]).reshape(-1)
            return [part[index] for index in range(8)] + [bias1]

        vectors = [small_params(layer) for layer in range(layers)]

        def own_width(vector):
            return lax.dynamic_slice_in_dim(vector, rank * width, width)

        docs = jnp.concatenate(docs)
        scale = pair_up(jnp.full((width,), HEAD ** (-0.5), F32), jnp.ones((width,), F32))

        kept = []
        rows_in = rows_low.astype(F32)
        for layer in range(layers):
            qk_w, v_w, out_w = attn_w[layer]
            bq, bv, bo, gain0, gain1, shift0, shift1, bias2, bias1 = vectors[layer]
            bias_qk = pair_up(own_width(bq), jnp.zeros((width,), F32))
            bias_v = own_width(bv)
            if layer:
                parts = team_rows(rows_low)
            qk, value = project_forward(parts, qk_w, v_w, bias_qk, scale, bias_v)
            if layer == 0:
                later = column[:, 4 * width + extra :]
                qk, value, second, ffn_part, later = together(qk, value, second, ffn_shard(1), later)
                attn_w[1], _ = gather_attn(*pieces_attn(*half_attn(later)))
                ffn_w[0] = gather_ffn(first), gather_ffn(second)
                ffn_part = column_ffn(jnp.concatenate(ffn_part, axis=0))
            context, logs = attend_forward(qk, value, docs)
            chip_rows = 2 * own_rows
            sums = chip_sums(
                lambda step: matmul(context[step * chip_rows : (step + 1) * chip_rows], out_w)
            )
            first_sum = rows_in + bo + team_sum(sums)
            first_norm = layer_norm(first_sum, gain0, shift0)
            norm_low = first_norm.astype(BF)
            if layer == 0:
                norm_low, ffn_part = together(norm_low, ffn_part)
                ffn_part = gather_ffn(ffn_part)
                ffn_w[1] = (ffn_part, ffn_part)
            chip_norm = (norm_low, swap_core(norm_low))
            if layer:
                chip_norm, grad_rows = together(chip_norm, grad_rows)
            reduced, give, *saved = ffn_forward(chip_norm, ffn_w[layer], bias1)
            second_sum = first_norm + (reduced + swap_core(give).astype(F32) + bias2)
            rows_in = layer_norm(second_sum, gain1, shift1)
            kept.append((parts, qk, value, context, logs, first_sum, saved, second_sum))
            rows_low = rows_in.astype(BF)
            if layer == 0:
                rows_low, cotangent = together(rows_low, cotangent)
                grad_rows = to_halves(cotangent).astype(F32)
        output_got = give_halves(rows_low)

        def own_first(mine):
            w1 = mine.reshape(layers, 2, rows1, WIDE)
            keep = jnp.where(core == 0, w1[:, :, :rows0], w1[:, :, rows0:])
            give = jnp.where(core == 0, w1[:, :, rows0:], w1[:, :, :rows0])
            got = swap_core(give)
            keep = jnp.swapaxes(keep, 1, 2).reshape(layers, rows0, -1, 1, units)
            got = jnp.swapaxes(got, 1, 2).reshape(layers, rows0, -1, 1, units)
            return by_core(keep, got, 3).reshape(layers, rows0, -1)

        def scatter_attn(first, second):
            first = first.reshape(n_fa, n_fb, n_s * rows0, -1)
            second = second.reshape(n_fa, n_fb, n_s * rows0, -1)
            first = scatter_shift(first, "fa", n_fa, 0).astype(BF)
            second = scatter_shift(second, "fb", n_fb, 1).astype(BF)
            return first, second

        def finish_attn(first, second):
            first = scatter_shift(first, "fb", n_fb, 0)
            second = scatter_shift(second, "fa", n_fa, 0)
            column = jnp.concatenate([first, second], axis=1).astype(BF)
            return column.reshape(n_s, rows0, -1)

        def own_attn(columns):
            pieces = lax.all_to_all(jnp.concatenate(columns, axis=-1), ("h", "m", "c"), 0, 0, tiled=True)
            pieces = jnp.sum(pieces.reshape((n_h, team, rows0, -1)).astype(F32), axis=0)

            def whole(first, count):
                return jnp.swapaxes(pieces[..., first : first + count], 0, 1).reshape(rows0, team * count)

            def matrices(first):
                qk = whole(first, 2 * width).reshape(rows0, team * pairs, 2, PAIR)
                query, key = qk[:, :, 0].reshape(rows0, WIDE), qk[:, :, 1].reshape(rows0, WIDE)
                first = first + 2 * width
                return jnp.stack([query, key, whole(first, width)]), whole(first + width, width)

            both = [matrices(4 * width * index) for index in range(layers)]
            return both, jnp.sum(pieces[..., 4 * width * layers :], axis=0)

        attn_columns = [None] * layers
        small_grads = [None] * layers
        for layer in reversed(range(layers)):
            parts, qk, value, context, logs, first_sum, saved, second_sum = kept[layer]
            (qk_w, v_w, out_w), ffn = attn_w[layer], ffn_w[layer]
            gain0, gain1 = vectors[layer][3], vectors[layer][4]
            grad_second, dgain1, dshift1 = layer_norm_back(grad_rows, second_sum, gain1)
            grad_low = grad_second.astype(BF)
            dbias2 = jnp.sum(grad_low, axis=0, dtype=F32)
            chip_low = (grad_low, swap_core(grad_low))
            if layer + 1 < layers:
                chip_low, attn_half = together(chip_low, attn_half)
            reduced, give, dbias1, dw1, dw2 = ffn_backward(chip_low, saved, ffn)
            if layer + 1 < layers:
                attn_columns[layer + 1] = finish_attn(*attn_half)
                ffn_last = jnp.concatenate(ffn_columns, axis=1)
            ffn_columns = [
                lax.psum_scatter(dw, ("fa", "fb"), scatter_dimension=0, tiled=True) for dw in (dw1, dw2)
            ]
            grad_first = grad_second + (reduced + swap_core(give).astype(F32))
            grad_sum, dgain0, dshift0 = layer_norm_back(grad_first, first_sum, gain0)
            grad_low = grad_sum.astype(BF)
            dbo = jnp.sum(grad_low, axis=0, dtype=F32)
            grads = team_rows(grad_low)
            if layer + 1 < layers:
                grads, ffn_last = together(grads, ffn_last)
                ffn_mine = scatter_shift(ffn_last, ("h", "m"), n_z, 0)
            grad_context, grad_out = output_backward(grads, context, out_w)
            grad_out = jnp.swapaxes(grad_out.reshape(width, team, width), 0, 1)
            grad_out = lax.all_to_all(grad_out, ("m", "c"), 0, 0, tiled=True).reshape(WIDE, width)
            dqk, dv = attend_backward(grad_context, qk, value, logs, docs)
            grad_qk, grad_v, own, give = project_backward(parts, dqk, dv, qk_w, v_w)
            if layer + 1 < layers:
                grad_qk, own, give, ffn_mine, attn_columns[layer + 1] = together(
                    grad_qk, own, give, ffn_mine, attn_columns[layer + 1]
                )
            else:
                own, give, output_got = together(own, give, output_got)
            sums = [own[step] + swap_core(give[step]).astype(F32) for step in range(n_m)]
            grad_rows = grad_sum + team_sum(sums)
            dbq = jnp.sum(dqk.reshape(-1, pairs, 2, PAIR)[:, :, 0], axis=0, dtype=F32)
            dbv = jnp.sum(dv, axis=0, dtype=F32)

            def spread(vector):
                blank = jnp.zeros((WIDE,), F32)
                return lax.dynamic_update_slice_in_dim(blank, vector.reshape(-1), rank * width, 0)

            dbias1 = dbias1.reshape(n_chip, 1, lots, rows0)
            dbias1 = by_core(dbias1, jnp.zeros_like(dbias1), 1).reshape(2 * n_chip, lots, rows0)
            dbias1 = jnp.swapaxes(dbias1, 0, 1).reshape(lots, WIDE)
            small_grads[layer] = jnp.concatenate(
                [
                    jnp.stack(
                        [spread(dbq), spread(dbv), dbo, dgain0, dgain1, dshift0, dshift1, dbias2]
                    ),
                    dbias1,
                ]
            )
            second = [grad_v, grad_out]
            if layer == 0:
                lanes = jnp.concatenate(small_grads, axis=0).T.astype(BF)
                second.append(jnp.pad(lanes, ((0, 0), (0, extra - layers * lanes_of))))
            attn_half = scatter_attn(grad_qk, jnp.concatenate(second, axis=1))
        grad_low = grad_rows.astype(BF)
        input_got = give_halves(grad_low)
        first = scatter_shift(ffn_columns[0], ("h", "m"), n_z, 0)
        second = scatter_shift(ffn_columns[1], ("h", "m"), n_z, 0)
        column, first, second, input_got = together(finish_attn(*attn_half), first, second, input_got)
        input_gradient = from_halves(grad_low, input_got).astype(F32)
        layer_output = from_halves(rows_low, output_got)
        w1_out = own_first(jnp.stack([first, ffn_mine[: 2 * rows1]]))
        w2_out = jnp.stack([second, ffn_mine[2 * rows1 :]])
        both, more = own_attn([attn_columns[1], column])

        more = more[:, : layers * lanes_of].T.reshape(layers, lanes_of, rows0)
        return (
            layer_output,
            input_gradient,
            jnp.stack([both[1][0], both[0][0]]),
            more[:, :2],
            jnp.stack([both[1][1], both[0][1]]),
            more[:, 2],
            more[:, 3:5],
            more[:, 5:7],
            w1_out,
            more[:, 8:].reshape(layers, units),
            w2_out,
            more[:, 7],
        )

    return body


def solution(mesh):
    n_f, n_s = mesh.shape["fsdp"], mesh.shape["seq"]
    sizes = (2, n_f // 2, 2, n_s // 4, 2)
    grid = Mesh(mesh.devices.reshape(sizes), ("fa", "fb", "h", "m", "c"))
    fsdp, seq = ("fa", "fb"), ("h", "m", "c")
    both = fsdp + seq
    tokens = P(fsdp, seq, None)
    third, second = P(None, None, both), P(None, both)
    weights = (
        P(None, None, both, None),
        third,
        P(None, both, None),
        second,
        third,
        third,
        P(None, both, None),
        second,
        P(None, both, None),
        second,
    )
    return jax.shard_map(
        make_body(*sizes[:4]),
        mesh=grid,
        in_specs=(tokens, P(fsdp, seq), tokens) + weights,
        out_specs=(tokens, tokens) + weights,
        check_vma=False,
    )
```
